512 devices in a mesh: blk: 16 (over x, y_lo, core), site: 32 (over z, y_hi).
Axes of the slice: x: 4, y: 8 (y_hi: 4, y_lo: 2; y = y_hi * 2 + y_lo), z: 8, core: 2. Of those that a mesh axis runs over, the one named last changes fastest.
Arguments:
- modes: bfloat16 [2, 1, 256, 12, 4096], P(None, None, 'blk', None, 'site'), may hold values from -0.5 to 0.5
- momenta: int32 [4, 3], replicated, may hold values from -2 to 2
Outputs:
- meson_field: float32 [128, 256, 256], P('site', 'blk')
The draws below stay inside these ranges and needn't reach their ends.
All inputs are finite; a program needn't handle non-finite values.
Results may differ from the reference program's by a relative error of at most 0.0027.
Values may be sent and summed in bfloat16 or wider, within the bound.
A program may use at most 128 MiB of HBM per device.

```python
import math
import jax
import jax.numpy as jnp
from jax import lax

NM = 256
LEXT = 48
NP = 4
NT = 1
SITES = 4096
BLOCKS = 16
BLOCK = 16


def with_ends(drawn, stream_key, smallest, largest):
    place = [jax.random.randint(jax.random.fold_in(stream_key, axis), (), 0, length) for axis, length in enumerate(drawn.shape)]
    longest = drawn.shape.index(max(drawn.shape))
    beside = place[:longest] + [(place[longest] + 1) % drawn.shape[longest]] + place[longest + 1:]
    return drawn.at[tuple(place)].set(smallest).at[tuple(beside)].set(largest)


def steps_of(key, shape, shards, low, largest):
    gain, own = 1.0, jax.random.fold_in(key, 6)
    for dim, shards_of in shards:
        draws = jnp.exp(jax.random.uniform(jax.random.fold_in(own, dim), (shards_of,), jnp.float32, low / len(shards), largest / len(shards)))
        gain = gain * jnp.repeat(draws, shape[dim] // shards_of).reshape([-1 if axis == dim else 1 for axis in range(len(shape))])
    return gain


def noise(key, shape, spread, bound, pieces=(), held_as=jnp.bfloat16):
    gain = steps_of(key, shape, pieces, -0.22, 0.18) if pieces else 1.0
    values = jax.random.normal(key, shape, jnp.float32) * spread * gain
    return jnp.minimum(jnp.maximum(values, -bound), bound).astype(held_as)


def setup_inputs(seed: int = 0) -> dict:
    seeds = jax.random.split(jax.random.key(seed), 3)
    return {
        "modes": noise(seeds[0], (2, NT, NM, 12, SITES), ((3 * SITES) ** -0.25), 0.5, ((2, 16), (4, 32))),
        "momenta": with_ends(jax.random.randint(seeds[1], (NP, 3), -2, 3), jax.random.fold_in(seeds[1], 1), -2, 2).astype(jnp.int32),
    }


TWO_PI = 2.0 * math.pi


def phase_table(momenta, first_site, site_count, extent):
    flat = first_site + jnp.arange(site_count, dtype=jnp.int32)
    coords = jnp.stack([flat % extent, (flat // extent) % extent, flat // (extent * extent)], 0)
    turns = jnp.mod(jnp.sum(momenta[:, :, None] * coords[None, :, :], axis=1), extent)
    angle = turns.astype(jnp.float32) * (TWO_PI / extent)
    return jnp.stack([jnp.cos(angle), jnp.sin(angle)], 1)


def reference(modes, momenta):
    half = BLOCKS // 2
    weights = phase_table(momenta, jnp.int32(0), SITES, LEXT)
    fields = modes.reshape(2, NT, NM, 4, 3, SITES)

    def one_pair(index):
        step = index // NP
        moment = index % NP
        field = lax.dynamic_index_in_dim(fields, step, 1, keepdims=False)
        weight = lax.dynamic_index_in_dim(weights, moment, 0, keepdims=False)
        phased = (field.astype(jnp.float32)[:, None] * weight[None, :, None, None, None, :]).astype(jnp.bfloat16)
        return jnp.einsum("awisxn,bjrxn->wabisjr", phased.astype(jnp.float32), field.astype(jnp.float32))

    products = lax.map(one_pair, jnp.arange(NT * NP, dtype=jnp.int32))
    real_part = products[:, :, 0, 0] + products[:, :, 1, 1]
    imag_part = products[:, :, 0, 1] - products[:, :, 1, 0]
    direct = jnp.stack([real_part[:, 0] + imag_part[:, 1], imag_part[:, 0] - real_part[:, 1]], 0)
    mirror = jnp.stack([real_part[:, 0] - imag_part[:, 1], -(imag_part[:, 0] + real_part[:, 1])], 0)
    direct = jnp.transpose(direct, (1, 3, 5, 0, 2, 4)).reshape(NT * NP * 32, NM, NM)
    mirror = jnp.transpose(mirror, (1, 5, 3, 0, 4, 2)).reshape(NT * NP * 32, NM, NM)
    owners = jnp.arange(NM) // BLOCK
    distance = jnp.mod(owners[:, None] - owners[None, :], BLOCKS)
    return jnp.where((distance <= half)[None], direct, mirror)
```

```python
import math

import jax
import jax.numpy as jnp
from jax import lax
from jax.experimental import pallas as pl
from jax.experimental.pallas import tpu as pltpu
from jax.sharding import PartitionSpec as P

LEXT = 48
TWO_PI = 2.0 * math.pi
MESH = pl.DeviceIdType.MESH
F32 = jnp.float32
BF16 = jnp.bfloat16
ZTYPE = jnp.bfloat16

NX, NY, NZ, NH = 4, 8, 8, 4
KEY = 768


def device(x, y, z, core):
    blk = x * 4 + lax.rem(y, 2) * 2 + core
    site = z * 4 + lax.div(y, 2)
    return (blk, site)


def remote(src, dst, send_sem, recv_sem, target):
    return pltpu.make_async_remote_copy(
        src_ref=src, dst_ref=dst, send_sem=send_sem, recv_sem=recv_sem,
        device_id=target, device_id_type=MESH,
    )


def kernel(
    modes_ref, mom_ref, out_ref,
    rows, cols, right_hi, right_lo, acc, tmp, zsend, zrecv, red, frecv,
    ring_s, ring_r, sib_s, sib_r, x_s, x_r, z_s, z_r, f_s, f_r,
):
    blk = lax.axis_index("blk")
    site = lax.axis_index("site")
    x = lax.div(blk, 4)
    yl = lax.rem(lax.div(blk, 2), 2)
    core = lax.rem(blk, 2)
    z = lax.div(site, 4)
    rho = lax.rem(site, 4)
    y = rho * 2 + yl
    other = 1 - core

    barrier = pltpu.get_barrier_semaphore()
    count = 0
    partners = []
    for dy in range(NY):
        for dc in range(2):
            if dy or dc:
                partners.append(device(x, lax.rem(y + dy, NY), z, lax.rem(core + dc, 2)))
    for dx in range(1, NX):
        partners.append(device(lax.rem(x + dx, NX), y, z, core))
    for dz in range(1, NZ):
        partners.append(device(x, y, lax.rem(z + dz, NZ), core))
    for target in partners:
        pl.semaphore_signal(barrier, inc=1, device_id=target, device_id_type=MESH)

    for c in range(2):
        for i in range(16):
            tmp[c, pl.ds(16 * i, 12), :] = modes_ref[c, 0, i].astype(F32)
    for c in range(2):
        for s in range(4):
            for a in range(3):
                piece = tmp[c, pl.ds(3 * s + a, 16, stride=16), :]
                lane = (c * 3 + a) * 128
                rows[y, core, pl.ds(16 * s, 16), pl.ds(lane, 128)] = piece.astype(BF16)

    row = lax.broadcasted_iota(jnp.int32, (8, 128), 0)
    lane = lax.broadcasted_iota(jnp.int32, (8, 128), 1)
    flat = ((z * 4 + (row & 3)) * 128 + lane).astype(F32)
    plane = jnp.floor((flat + 0.5) * (1.0 / (LEXT * LEXT)))
    line = jnp.floor((flat + 0.5) * (1.0 / LEXT))
    coords = (flat - LEXT * line, line - LEXT * plane, plane)
    phases = []
    for k in range(4):
        turns = sum(mom_ref[k, d].astype(F32) * coords[d] for d in range(3))
        turns = turns - LEXT * jnp.floor((turns + 0.5) * (1.0 / LEXT))
        angle = turns * (TWO_PI / LEXT)
        phases.append((jnp.cos(angle), jnp.sin(angle)))
    for k in range(4):
        tmp[0, pl.ds(8 * k, 8), :] = phases[k][0]
        tmp[1, pl.ds(8 * k, 8), :] = phases[k][1]

    pl.semaphore_wait(barrier, len(partners))

    sign = (1, NY - 1)

    def ring(d, t, h):
        src = rows.at[lax.rem(y + (NY - sign[d]) * (t - 1), NY), core, pl.ds(32 * h, 32), :]
        target = device(x, lax.rem(y + sign[d], NY), z, core)
        return remote(src, src, ring_s.at[d, t - 1, h], ring_r.at[d, t - 1, h], target)

    def ring_in(d, t, h):
        dst = rows.at[lax.rem(y + (NY - sign[d]) * t, NY), core, pl.ds(32 * h, 32), :]
        target = device(x, lax.rem(y + sign[d], NY), z, core)
        return remote(dst, dst, ring_s.at[d, t - 1, h], ring_r.at[d, t - 1, h], target)

    def place(d, t):
        return 0 if t == 0 else 1 + d * 4 + t - 1

    def sib(d, t, h):
        src = rows.at[lax.rem(y + (NY - sign[d]) * t, NY), core, pl.ds(32 * h, 32), :]
        at = place(d, t)
        return remote(src, src, sib_s.at[at, h], sib_r.at[at, h], device(x, y, z, other))

    def sib_in(d, t, h):
        dst = rows.at[lax.rem(y + (NY - sign[d]) * t, NY), other, pl.ds(32 * h, 32), :]
        at = place(d, t)
        return remote(dst, dst, sib_s.at[at, h], sib_r.at[at, h], device(x, y, z, other))

    def x_out(dx, e):
        hi = lax.rem(rho + e, NH)
        src = rows.at[hi * 2 + yl, core, pl.ds(pl.multiple_of(rho * 16, 16), 16), :]
        target = device(lax.rem(x + dx, NX), y, z, core)
        return remote(src, cols.at[x, hi], x_s.at[dx - 1, e], x_r.at[dx - 1, e], target)

    def x_in(dx, e):
        hi = lax.rem(rho + e, NH)
        dst = cols.at[lax.rem(x + NX - dx, NX), hi]
        target = device(lax.rem(x + dx, NX), y, z, core)
        return remote(dst, dst, x_s.at[dx - 1, e], x_r.at[dx - 1, e], target)

    def x_start(e):
        for dx in (2, 1, 3):
            x_out(dx, e).start()
        hi = lax.rem(rho + e, NH)
        cols[x, hi] = rows[hi * 2 + yl, core, pl.ds(pl.multiple_of(rho * 16, 16), 16), :]

    def multiply(e):
        hi = lax.rem(rho + e, NH)
        for dx in range(1, NX):
            x_in(dx, e).wait_recv()
        for k in range(4):
            cos = tmp[0, pl.ds(8 * k + hi, 1), :]
            sin = tmp[1, pl.ds(8 * k + hi, 1), :]
            for xs in range(NX):
                for a in range(3):
                    ur = cols[xs, hi, :, pl.ds(a * 128, 128)].astype(F32)
                    ui = cols[xs, hi, :, pl.ds((3 + a) * 128, 128)].astype(F32)
                    qr = ur * cos + ui * sin
                    qi = ui * cos - ur * sin
                    hr, hm = qr.astype(BF16), qi.astype(BF16)
                    lr = (qr - hr.astype(F32)).astype(BF16)
                    lm = (qi - hm.astype(F32)).astype(BF16)
                    at = k * 128 + (xs % 2) * 64 + (xs // 2) * 16
                    for buffer, re, im in ((right_hi, hr, hm), (right_lo, lr, lm)):
                        buffer[pl.ds(at, 16), pl.ds(a * 128, 128)] = re
                        buffer[pl.ds(at, 16), pl.ds((3 + a) * 128, 128)] = im
                        buffer[pl.ds(at + 32, 16), pl.ds(a * 128, 128)] = im
                        buffer[pl.ds(at + 32, 16), pl.ds((3 + a) * 128, 128)] = -re
        dims = (((1,), (1,)), ((), ()))
        left = rows[pl.ds(hi * 2, 2)].reshape(256, KEY)
        for k in range(4):
            part = lax.dot_general(left, right_hi[pl.ds(128 * k, 128), :], dims, preferred_element_type=F32)
            part += lax.dot_general(left, right_lo[pl.ds(128 * k, 128), :], dims, preferred_element_type=F32)
            if e == 0:
                acc[k] = part
            else:
                acc[k] += part

    started = []
    for h in range(2):
        for d in range(2):
            ring(d, 1, h).start()
    for h in range(2):
        sib(0, 0, h).start()
    x_start(0)
    for h in range(2):
        for d in range(2):
            ring_in(d, 1, h).wait_recv()
            ring(d, 2, h).start()
            sib(d, 1, h).start()
    for h in range(2):
        for d in range(2):
            ring_in(d, 2, h).wait_recv()
            ring(d, 3, h).start()
            sib(d, 2, h).start()
    x_start(1)
    x_start(3)
    for h in range(2):
        sib_in(0, 0, h).wait_recv()
        for d in range(2):
            sib_in(d, 1, h).wait_recv()
    multiply(0)
    for h in range(2):
        for d in range(2):
            ring_in(d, 3, h).wait_recv()
            if h == d:
                ring(d, 4, h).start()
            sib(d, 3, h).start()
    for h in range(2):
        for d in range(2):
            sib_in(d, 2, h).wait_recv()
            sib_in(d, 3, h).wait_recv()
    multiply(1)
    for d in range(2):
        ring_in(d, 4, d).wait_recv()
        sib(d, 4, d).start()
    x_start(2)
    multiply(3)
    for d in range(2):
        sib_in(d, 4, d).wait_recv()
    multiply(2)

    for zz in range(NZ):
        for q in range(4):
            zsend[zz, pl.ds(32 * q, 32), :] = acc[zz // 2, pl.ds(64 * q + 32 * (zz % 2), 32), :].astype(ZTYPE)

    def z_out(dz):
        to = lax.rem(z + dz, NZ)
        return remote(zsend.at[to], zrecv.at[dz - 1], z_s.at[dz - 1], z_r.at[dz - 1], device(x, y, to, core))

    for dz in (4, 3, 5, 2, 6, 1, 7):
        z_out(dz).start()
    half = pl.multiple_of(lax.rem(z, 2) * 32, 32)
    for q in range(4):
        red[pl.ds(32 * q, 32), :] = acc[lax.div(z, 2), pl.ds(64 * q + half, 32), :]
    for dz in (1, 7, 2, 6, 3, 5, 4):
        z_out(dz).wait_recv()
        red[...] += zrecv[dz - 1].astype(F32)

    mine = lax.rem(rho, 2) * 4 + yl * 2 + core

    def f_out(q, sp):
        to = device(x, (sp * 2 + lax.div(rho, 2)) * 2 + q // 2, z, q % 2)
        src = red.at[pl.ds(32 * q + 16 * sp, 16), :]
        return remote(src, frecv.at[mine], f_s.at[q * 2 + sp], f_r.at[mine], to)

    def f_self(q, sp):
        return (sp * 2 + lax.div(rho, 2) == rho) & (yl == q // 2) & (core == q % 2)

    def f_in(b, q):
        dst = frecv.at[b * 4 + q]
        source = device(x, (lax.rem(rho, 2) * 2 + b) * 2 + q // 2, z, q % 2)
        return remote(dst, dst, f_s.at[b * 4 + q], f_r.at[b * 4 + q], source)

    def f_self_in(b, q):
        return (lax.rem(rho, 2) * 2 + b == rho) & (yl == q // 2) & (core == q % 2)

    for sp in range(2):
        for q in range(4):
            here = f_self(q, sp)

            @pl.when(jnp.logical_not(here))
            def _():
                f_out(q, sp).start()

            @pl.when(here)
            def _():
                frecv[mine] = red[pl.ds(32 * q + 16 * sp, 16), :]

    for b in range(2):
        for q in range(4):

            @pl.when(jnp.logical_not(f_self_in(b, q)))
            def _():
                f_in(b, q).wait_recv()

    group = lax.div(lax.rem(lax.broadcasted_iota(jnp.int32, (16, 128), 1), 64), 16)
    for b in range(2):
        pieces = [frecv[b * 4 + q] for q in range(4)]
        for c in range(2):
            for v in range(2):
                m = c * 2 + v
                total = pieces[m]
                for q in range(4):
                    if q != m:
                        moved = pltpu.roll(pieces[q], ((q - m) * 16) % 128, 1)
                        total = jnp.where(group == q, moved, total)
                out_ref[b * 2 + c, :, pl.ds(128 * v, 128)] = total

    for h in range(2):
        sib(0, 0, h).wait_send()
        for d in range(2):
            for t in (1, 2, 3):
                ring(d, t, h).wait_send()
                sib(d, t, h).wait_send()
    for d in range(2):
        ring(d, 4, d).wait_send()
        sib(d, 4, d).wait_send()
    for e in range(4):
        for dx in range(1, NX):
            x_out(dx, e).wait_send()
    for dz in range(1, NZ):
        z_out(dz).wait_send()
    for sp in range(2):
        for q in range(4):

            @pl.when(jnp.logical_not(f_self(q, sp)))
            def _():
                f_out(q, sp).wait_send()


def shards(modes, momenta):
    dma = pltpu.SemaphoreType.DMA
    return pl.pallas_call(
        kernel,
        out_shape=jax.ShapeDtypeStruct((4, 16, 256), F32),
        in_specs=[
            pl.BlockSpec(memory_space=pltpu.VMEM),
            pl.BlockSpec(memory_space=pltpu.SMEM),
        ],
        out_specs=pl.BlockSpec(memory_space=pltpu.VMEM),
        scratch_shapes=[
            pltpu.VMEM((NY, 2, 64, KEY), BF16),
            pltpu.VMEM((NX, NH, 16, KEY), BF16),
            pltpu.VMEM((512, KEY), BF16),
            pltpu.VMEM((512, KEY), BF16),
            pltpu.VMEM((4, 256, 128), F32),
            pltpu.VMEM((2, 256, 128), F32),
            pltpu.VMEM((NZ, 128, 128), ZTYPE),
            pltpu.VMEM((NZ - 1, 128, 128), ZTYPE),
            pltpu.VMEM((128, 128), F32),
            pltpu.VMEM((8, 16, 128), F32),
            dma((2, 4, 2)), dma((2, 4, 2)),
            dma((9, 2)), dma((9, 2)),
            dma((NX - 1, NH)), dma((NX - 1, NH)),
            dma((NZ - 1,)), dma((NZ - 1,)),
            dma((8,)), dma((8,)),
        ],
        compiler_params=pltpu.CompilerParams(
            collective_id=0, has_side_effects=True, vmem_limit_bytes=32 * 1024 * 1024
        ),
    )(modes, momenta)


def solution(mesh):
    placed = (P(None, None, "blk", None, "site"), P())
    return jax.shard_map(
        shards, mesh=mesh, in_specs=placed, out_specs=P("site", "blk", None), check_vma=False
    )
```

```python
import math

import jax
import jax.numpy as jnp
from jax import lax
from jax.experimental import pallas as pl
from jax.experimental.pallas import tpu as pltpu
from jax.sharding import PartitionSpec as P

LEXT = 48
TWO_PI = 2.0 * math.pi
MESH = pl.DeviceIdType.MESH
F32 = jnp.float32
BF16 = jnp.bfloat16

NX, NZ, NH = 4, 8, 4
KEY = 768
ROWS = (((1,), (1,)), ((), ()))


def remote(src, dst, send_sem, recv_sem, target):
    return pltpu.make_async_remote_copy(
        src_ref=src, dst_ref=dst, send_sem=send_sem, recv_sem=recv_sem,
        device_id=target, device_id_type=MESH,
    )


def spin_of(hi):
    return (1 - lax.rem(hi, 2)) * 2 + lax.div(hi, 2)


def spin_rows(spin):
    return pl.ds(pl.multiple_of(spin * 16, 16), 16)


def kernel(
    modes_ref, mom_ref, out_ref,
    stage, mom, rows, cols, left_hi, left_lo, acc, wave, zsend, zrecv, red,
    in_s, y_s, y_r, o_s, o_r, x_s, x_r, s_s, s_r, z_s, z_r, f_s, f_r,
):
    blk = lax.axis_index("blk")
    site = lax.axis_index("site")
    x = lax.div(blk, 4)
    yl = lax.rem(lax.div(blk, 2), 2)
    core = lax.rem(blk, 2)
    z = lax.div(site, 4)
    rho = lax.rem(site, 4)
    spin = spin_of(rho)

    def device(x, yl, core, z, hi):
        return (x * 4 + yl * 2 + core, z * 4 + hi)

    def block(x, yl, core):
        return x * 4 + yl * 2 + core

    def lane_of(o):
        return yl if o == 0 else 1 - yl

    def up(hi, e):
        return lax.rem(hi + e, NH)

    barrier = pltpu.get_barrier_semaphore()
    partners = [device(x, lane_of(o), core, z, up(rho, e)) for e in range(NH) for o in range(2) if e or o]
    partners += [device(lax.rem(x + dx, NX), yl, core, z, rho) for dx in range(1, NX)]
    partners += [device(x, yl, core, lax.rem(z + dz, NZ), rho) for dz in range(1, NZ)]
    partners += [device(x, yl, 1 - core, z, rho)]
    for target in partners:
        pl.semaphore_signal(barrier, inc=1, device_id=target, device_id_type=MESH)
    get_modes = pltpu.make_async_copy(modes_ref, stage, in_s.at[0])
    get_modes.start()
    get_mom = pltpu.make_async_copy(mom_ref, mom, in_s.at[1])
    get_mom.start()

    get_modes.wait()
    for c in range(2):
        for s in range(4):
            for a in range(3):
                rows[rho, pl.ds(16 * s, 16), pl.ds((c * 3 + a) * 128, 128)] = stage[c, 0, 3 * s + a]
    cols[rho, blk] = rows[rho, spin_rows(spin), :]

    def y_out(e, j):
        to = up(rho, e)
        piece = rows.at[rho, spin_rows(lax.rem(spin_of(to) + j, 4)), :]
        return remote(piece, piece, y_s.at[e - 1, j], y_r.at[e - 1, j], device(x, yl, core, z, to))

    def y_in(e, j):
        piece = rows.at[up(rho, NH - e), spin_rows(lax.rem(spin + j, 4)), :]
        return remote(piece, piece, y_s.at[e - 1, j], y_r.at[e - 1, j], device(x, yl, core, z, up(rho, NH - e)))

    def o_out(e):
        to = up(rho, e)
        piece = rows.at[rho, spin_rows(spin_of(to)), :]
        return remote(piece, cols.at[rho, blk], o_s.at[e], o_r.at[e], device(x, 1 - yl, core, z, to))

    def o_in(e):
        hi = up(rho, NH - e)
        piece = cols.at[hi, block(x, 1 - yl, core)]
        return remote(piece, piece, o_s.at[e], o_r.at[e], device(x, 1 - yl, core, z, hi))

    def x_out(dx, e, o):
        piece = cols.at[up(rho, NH - e), block(x, lane_of(o), core)]
        to = device(lax.rem(x + dx, NX), yl, core, z, rho)
        return remote(piece, piece, x_s.at[dx - 1, e, o], x_r.at[dx - 1, e, o], to)

    def x_in(dx, e, o):
        far = lax.rem(x + NX - dx, NX)
        piece = cols.at[up(rho, NH - e), block(far, lane_of(o), core)]
        return remote(piece, piece, x_s.at[dx - 1, e, o], x_r.at[dx - 1, e, o], device(far, yl, core, z, rho))

    def s_copy(dx, e, o, side):
        far = lax.rem(x + NX - dx, NX)
        piece = cols.at[up(rho, NH - e), block(far, lane_of(o), side)]
        return remote(piece, piece, s_s.at[dx, e, o], s_r.at[dx, e, o], device(x, yl, 1 - core, z, rho))

    def spread(e, o):
        for dx in (2, 1, 3):
            x_out(dx, e, o).start()
        s_copy(0, e, o, core).start()

    pl.semaphore_wait(barrier, len(partners))
    y_out(2, 0).start()
    o_out(2).start()
    for e in (1, 3):
        o_out(e).start()
        y_out(e, 0).start()
    o_out(0).start()
    spread(0, 0)
    for j in range(1, 4):
        for e in (2, 1, 3):
            y_out(e, j).start()

    get_mom.wait()
    row = lax.broadcasted_iota(jnp.int32, (8, 128), 0)
    lane = lax.broadcasted_iota(jnp.int32, (8, 128), 1)
    flat = ((z * 4 + (row & 3)) * 128 + lane).astype(F32)
    plane = jnp.floor((flat + 0.5) * (1.0 / (LEXT * LEXT)))
    line = jnp.floor((flat + 0.5) * (1.0 / LEXT))
    coords = (flat - LEXT * line, line - LEXT * plane, plane)
    for k in range(4):
        turns = sum(mom[k, d].astype(F32) * coords[d] for d in range(3))
        turns = turns - LEXT * jnp.floor((turns + 0.5) * (1.0 / LEXT))
        angle = turns * (TWO_PI / LEXT)
        wave[0, pl.ds(8 * k, 8), :] = jnp.cos(angle)
        wave[1, pl.ds(8 * k, 8), :] = jnp.sin(angle)

    def prepare(e):
        hi = up(rho, NH - e)
        for k in range(4):
            cos = wave[0, pl.ds(8 * k + hi, 1), :]
            sin = wave[1, pl.ds(8 * k + hi, 1), :]
            for s in range(4):
                for a in range(3):
                    ur = rows[hi, pl.ds(16 * s, 16), pl.ds(a * 128, 128)].astype(F32)
                    ui = rows[hi, pl.ds(16 * s, 16), pl.ds((3 + a) * 128, 128)].astype(F32)
                    re = ur * cos - ui * sin
                    im = ui * cos + ur * sin
                    re_hi, im_hi = re.astype(BF16), im.astype(BF16)
                    re_lo = (re - re_hi.astype(F32)).astype(BF16)
                    im_lo = (im - im_hi.astype(F32)).astype(BF16)
                    at = k * 128 + s * 32
                    for left, first, second in ((left_hi, re_hi, im_hi), (left_lo, re_lo, im_lo)):
                        left[e, pl.ds(at, 16), pl.ds(a * 128, 128)] = first
                        left[e, pl.ds(at, 16), pl.ds((3 + a) * 128, 128)] = second
                        left[e, pl.ds(at + 16, 16), pl.ds(a * 128, 128)] = -second
                        left[e, pl.ds(at + 16, 16), pl.ds((3 + a) * 128, 128)] = first

    def multiply(e, last=False):
        right = cols[up(rho, NH - e)].reshape(256, KEY)
        for k in range(4):
            at = pl.ds(128 * k, 128)
            part = lax.dot_general(left_hi[e, at, :], right, ROWS, preferred_element_type=F32)
            part += lax.dot_general(left_lo[e, at, :], right, ROWS, preferred_element_type=F32)
            if e != 0:
                part += acc[at, :]
            acc[at, :] = part
            if last:
                zsend[2 * k] = part[:64].astype(BF16)
                zsend[2 * k + 1] = part[64:].astype(BF16)

    def relay(e, o):
        for dx in (1, 3, 2):
            x_in(dx, e, o).wait_recv()
            s_copy(dx, e, o, core).start()

    def whole(e):
        for dx in range(NX):
            for o in range(2):
                s_copy(dx, e, o, 1 - core).wait_recv()

    prepare(0)
    o_in(0).wait_recv()
    spread(0, 1)
    for e in (1, 3):
        o_in(e).wait_recv()
        spread(e, 1)
        y_in(e, 0).wait_recv()
        cols[up(rho, NH - e), blk] = rows[up(rho, NH - e), spin_rows(spin), :]
        spread(e, 0)
    o_in(2).wait_recv()
    spread(2, 1)
    y_in(2, 0).wait_recv()
    cols[up(rho, 2), blk] = rows[up(rho, 2), spin_rows(spin), :]
    spread(2, 0)
    relay(0, 0)
    relay(0, 1)
    for e in (1, 3):
        for j in range(1, 4):
            y_in(e, j).wait_recv()
        prepare(e)
        relay(e, 1)
        relay(e, 0)
    relay(2, 1)
    relay(2, 0)
    whole(0)
    multiply(0)
    for j in range(1, 4):
        y_in(2, j).wait_recv()
    prepare(2)
    for e in (1, 3):
        whole(e)
        multiply(e)
    whole(2)
    multiply(2, last=True)

    def z_out(dz):
        to = lax.rem(z + dz, NZ)
        return remote(zsend.at[to], zrecv.at[dz - 1], z_s.at[dz - 1], z_r.at[dz - 1], device(x, yl, core, to, rho))

    for dz in (4, 3, 5, 2, 6, 1, 7):
        z_out(dz).start()
    total = acc[pl.ds(pl.multiple_of(64 * z, 64), 64), :]
    for dz in (1, 7, 2, 6, 3, 5, 4):
        z_out(dz).wait_recv()
        total += zrecv[dz - 1].astype(F32)
    for sp in range(2):
        for c in range(2):
            red[sp, c] = total[32 * sp + 16 * c:32 * sp + 16 * c + 16]

    def f_out(sp):
        to = device(x, yl, core, z, sp * 2 + 1 - lax.rem(rho, 2))
        half = lax.div(rho, 2)
        return remote(red.at[sp], out_ref.at[pl.ds(half * 2, 2)], f_s.at[sp], f_r.at[half], to)

    def f_in(half):
        source = device(x, yl, core, z, half * 2 + 1 - lax.rem(rho, 2))
        piece = out_ref.at[pl.ds(half * 2, 2)]
        return remote(piece, piece, f_s.at[half], f_r.at[half], source)

    for sp in range(2):
        f_out(sp).start()

    for e in range(NH):
        o_out(e).wait_send()
        for o in range(2):
            for dx in range(1, NX):
                x_out(dx, e, o).wait_send()
            for dx in range(NX):
                s_copy(dx, e, o, core).wait_send()
        if e:
            for j in range(4):
                y_out(e, j).wait_send()
    for dz in range(1, NZ):
        z_out(dz).wait_send()
    for half in range(2):
        f_in(half).wait_recv()
    for sp in range(2):
        f_out(sp).wait_send()


def shards(modes, momenta):
    dma = pltpu.SemaphoreType.DMA
    return pl.pallas_call(
        kernel,
        out_shape=jax.ShapeDtypeStruct((4, 16, 256), F32),
        in_specs=[
            pl.BlockSpec(memory_space=pl.ANY),
            pl.BlockSpec(memory_space=pl.ANY),
        ],
        out_specs=pl.BlockSpec(memory_space=pltpu.VMEM),
        scratch_shapes=[
            pltpu.VMEM((2, 1, 12, 16, 128), BF16),
            pltpu.SMEM((4, 3), jnp.int32),
            pltpu.VMEM((NH, 64, KEY), BF16),
            pltpu.VMEM((NH, 16, 16, KEY), BF16),
            pltpu.VMEM((NH, 512, KEY), BF16),
            pltpu.VMEM((NH, 512, KEY), BF16),
            pltpu.VMEM((512, 256), F32),
            pltpu.VMEM((2, 32, 128), F32),
            pltpu.VMEM((NZ, 64, 256), BF16),
            pltpu.VMEM((NZ - 1, 64, 256), BF16),
            pltpu.VMEM((2, 2, 16, 256), F32),
            dma((2,)),
            dma((NH - 1, 4)), dma((NH - 1, 4)),
            dma((NH,)), dma((NH,)),
            dma((NX - 1, NH, 2)), dma((NX - 1, NH, 2)),
            dma((NX, NH, 2)), dma((NX, NH, 2)),
            dma((NZ - 1,)), dma((NZ - 1,)),
            dma((2,)), dma((2,)),
        ],
        compiler_params=pltpu.CompilerParams(
            collective_id=0, has_side_effects=True, vmem_limit_bytes=56 * 1024 * 1024
        ),
    )(jnp.transpose(modes, (0, 1, 3, 2, 4)), momenta)


def solution(mesh):
    placed = (P(None, None, "blk", None, "site"), P())
    return jax.shard_map(
        shards, mesh=mesh, in_specs=placed, out_specs=P("site", "blk", None), check_vma=False
    )
```

```python
import math

import jax
import jax.numpy as jnp
from jax import lax
from jax.experimental import pallas as pl
from jax.experimental.pallas import tpu as pltpu
from jax.sharding import PartitionSpec as P

LEXT = 48
TWO_PI = 2.0 * math.pi
MESH = pl.DeviceIdType.MESH
F32 = jnp.float32
BF16 = jnp.bfloat16

NX, NZ, NH = 4, 8, 4
KEY = 768
ROWS = (((1,), (1,)), ((), ()))


def remote(src, dst, send_sem, recv_sem, target):
    return pltpu.make_async_remote_copy(
        src_ref=src, dst_ref=dst, send_sem=send_sem, recv_sem=recv_sem,
        device_id=target, device_id_type=MESH,
    )


def flip(place):
    return place + 1 - 2 * lax.rem(place, 2)


def spin_rows(spin):
    return pl.ds(pl.multiple_of(spin * 16, 16), 16)


def kernel(
    modes_ref, mom_ref, out_ref,
    stage, mom, rows, cols, left_hi, left_lo, acc, wave, zsend, zrecv,
    hand, in_s, g_s, g_r, a_s, a_r, x_s, x_r, s_s, s_r, z_s, z_r,
):
    blk = lax.axis_index("blk")
    site = lax.axis_index("site")
    x = lax.div(blk, 4)
    yl = lax.rem(lax.div(blk, 2), 2)
    core = lax.rem(blk, 2)
    z = lax.div(site, 4)
    rho = lax.rem(site, 4)

    def hi_of(e):
        return flip(rho) if e % 2 else rho

    def z_of(e):
        return flip(z) if e // 2 else z

    def spin_of(e):
        return (1 - lax.rem(hi_of(e), 2)) * 2 + lax.rem(z_of(e), 2)

    spin = spin_of(0)

    def device(x, yl, core, z, hi):
        return (x * 4 + yl * 2 + core, z * 4 + hi)

    def block(x, yl, core):
        return x * 4 + yl * 2 + core

    def lane_of(o):
        return yl if o == 0 else 1 - yl

    barrier = pltpu.get_barrier_semaphore()
    partners = [device(x, yl, 1 - core, z, rho), device(x, yl, core, z_of(3), hi_of(3))]
    partners += [device(lax.rem(x + dx, NX), yl, core, z, rho) for dx in range(1, NX)]
    partners += [device(x, 1 - yl, core, z_of(e), hi_of(e)) for e in range(NH)]
    along_z = [device(x, yl, core, lax.rem(z + dz, NZ), rho) for dz in (1, NZ - 1)]
    along_y = [device(x, yl, core, z, lax.rem(rho + dh, NH)) for dh in (1, NH - 1)]
    partners += along_z + along_y
    for target in partners:
        pl.semaphore_signal(barrier, inc=1, device_id=target, device_id_type=MESH)
    get_modes = pltpu.make_async_copy(modes_ref, stage, in_s.at[0])
    get_modes.start()
    get_mom = pltpu.make_async_copy(mom_ref, mom, in_s.at[1])
    get_mom.start()

    get_modes.wait()
    for c in range(2):
        for s in range(4):
            for a in range(3):
                rows[0, pl.ds(16 * s, 16), pl.ds((c * 3 + a) * 128, 128)] = stage[c, 0, 3 * s + a]

    def gather(e, spin_e, e_from, to, way=0):
        return remote(
            rows.at[e_from, spin_rows(spin_e), :], rows.at[e, spin_rows(spin_e), :],
            g_s.at[e - 1 + way, spin_e], g_r.at[e - 1, spin_e], to,
        )

    def y_out(j):
        return gather(1, spin_of(j), 0, device(x, yl, core, z, flip(rho)))

    def z_out(j):
        return gather(2, spin_of(j), 0, device(x, yl, core, flip(z), rho))

    def d_out():
        return gather(3, spin_of(3), 0, device(x, yl, core, z_of(3), hi_of(3)), 1)

    def f_out(j):
        return gather(3, spin_of(j), 1, device(x, yl, core, flip(z), rho))

    def g_in(e, j):
        to = device(x, yl, core, flip(z), rho) if e > 1 else device(x, yl, core, z, flip(rho))
        return gather(e, spin_of(j), e, to)

    def a_out(e):
        to = device(x, 1 - yl, core, z_of(e), hi_of(e))
        return remote(rows.at[0, spin_rows(spin_of(e)), :], cols.at[e, blk], a_s.at[e], a_r.at[e], to)

    def a_in(e):
        piece = cols.at[e, block(x, 1 - yl, core)]
        return remote(piece, piece, a_s.at[e], a_r.at[e], device(x, 1 - yl, core, z_of(e), hi_of(e)))

    def x_out(dx, e, o):
        piece = cols.at[e, block(x, lane_of(o), core)]
        to = device(lax.rem(x + dx, NX), yl, core, z, rho)
        return remote(piece, piece, x_s.at[dx - 1, e, o], x_r.at[dx - 1, e, o], to)

    def x_in(dx, e, o):
        far = lax.rem(x + NX - dx, NX)
        piece = cols.at[e, block(far, lane_of(o), core)]
        return remote(piece, piece, x_s.at[dx - 1, e, o], x_r.at[dx - 1, e, o], device(far, yl, core, z, rho))

    def s_copy(dx, e, o, side):
        piece = cols.at[e, block(lax.rem(x + NX - dx, NX), lane_of(o), side)]
        return remote(piece, piece, s_s.at[dx, e, o], s_r.at[dx, e, o], device(x, yl, 1 - core, z, rho))

    def spread(e, o):
        if o == 0:
            cols[e, blk] = rows[e, spin_rows(spin), :]
        for dx in (2, 1, 3):
            x_out(dx, e, o).start()
        s_copy(0, e, o, core).start()

    def relay(e, o):
        for dx in (1, 3, 2):
            x_in(dx, e, o).wait_recv()
            s_copy(dx, e, o, core).start()

    def whole(e):
        for dx in range(NX):
            for o in range(2):
                s_copy(dx, e, o, 1 - core).wait_recv()

    def prepare(e):
        for k in range(4):
            cos = wave[0, pl.ds(8 * k + e, 1), :]
            sin = wave[1, pl.ds(8 * k + e, 1), :]
            for s in range(4):
                for a in range(3):
                    ur = rows[e, pl.ds(16 * s, 16), pl.ds(a * 128, 128)].astype(F32)
                    ui = rows[e, pl.ds(16 * s, 16), pl.ds((3 + a) * 128, 128)].astype(F32)
                    re = ur * cos - ui * sin
                    im = ui * cos + ur * sin
                    re_hi, im_hi = re.astype(BF16), im.astype(BF16)
                    re_lo = (re - re_hi.astype(F32)).astype(BF16)
                    im_lo = (im - im_hi.astype(F32)).astype(BF16)
                    at = k * 128 + s * 32
                    for left, first, second in ((left_hi, re_hi, im_hi), (left_lo, re_lo, im_lo)):
                        left[e, pl.ds(at, 16), pl.ds(a * 128, 128)] = first
                        left[e, pl.ds(at, 16), pl.ds((3 + a) * 128, 128)] = second
                        left[e, pl.ds(at + 16, 16), pl.ds(a * 128, 128)] = -second
                        left[e, pl.ds(at + 16, 16), pl.ds((3 + a) * 128, 128)] = first

    def multiply(e, first=False, last=False):
        right = cols[e].reshape(256, KEY)
        for k in range(4):
            at = pl.ds(128 * k, 128)
            part = lax.dot_general(left_hi[e, at, :], right, ROWS, preferred_element_type=F32)
            part += lax.dot_general(left_lo[e, at, :], right, ROWS, preferred_element_type=F32)
            if not first:
                part += acc[at, :]
            if last:
                for half in range(4):
                    zsend[2 * k + half // 2, half % 2] = part[32 * half:32 * half + 32].astype(BF16)
            else:
                acc[at, :] = part

    def tell(turn):
        for side, to in enumerate(along_z if turn < 3 else along_y):
            pl.semaphore_signal(hand.at[turn, side], inc=1, device_id=to, device_id_type=MESH)

    def hear(turn):
        for side in range(2):
            pl.semaphore_wait(hand.at[turn, side], 1)

    pl.semaphore_wait(barrier, len(partners))
    y_out(1).start()
    z_out(2).start()
    a_out(0).start()
    spread(0, 0)
    d_out().start()
    a_out(3).start()
    a_out(1).start()
    a_out(2).start()
    tell(0)
    y_out(3).start()
    z_out(0).start()
    y_out(0).start()
    z_out(1).start()
    y_out(2).start()
    z_out(3).start()

    get_mom.wait()
    row = lax.broadcasted_iota(jnp.int32, (8, 128), 0)
    lane = lax.broadcasted_iota(jnp.int32, (8, 128), 1)
    hi_row = rho + (row & 1) * (flip(rho) - rho)
    z_row = z + (lax.shift_right_logical(row, 1) & 1) * (flip(z) - z)
    flat = ((z_row * 4 + hi_row) * 128 + lane).astype(F32)
    plane = jnp.floor((flat + 0.5) * (1.0 / (LEXT * LEXT)))
    line = jnp.floor((flat + 0.5) * (1.0 / LEXT))
    coords = (flat - LEXT * line, line - LEXT * plane, plane)
    for k in range(4):
        turns = sum(mom[k, d].astype(F32) * coords[d] for d in range(3))
        turns = turns - LEXT * jnp.floor((turns + 0.5) * (1.0 / LEXT))
        angle = turns * (TWO_PI / LEXT)
        wave[0, pl.ds(8 * k, 8), :] = jnp.cos(angle)
        wave[1, pl.ds(8 * k, 8), :] = jnp.sin(angle)

    prepare(0)
    a_in(0).wait_recv()
    spread(0, 1)
    g_in(2, 0).wait_recv()
    spread(2, 0)
    g_in(1, 0).wait_recv()
    spread(1, 0)
    a_in(2).wait_recv()
    spread(2, 1)
    a_in(1).wait_recv()
    spread(1, 1)
    g_in(3, 0).wait_recv()
    spread(3, 0)
    a_in(3).wait_recv()
    spread(3, 1)
    f_out(0).start()
    hear(0)
    tell(1)
    for j in (1, 3):
        g_in(1, j).wait_recv()
        f_out(j).start()
    g_in(1, 2).wait_recv()
    relay(0, 0)
    relay(0, 1)
    hear(1)
    tell(2)
    prepare(1)
    relay(2, 0)
    relay(1, 0)
    for j in (1, 2, 3):
        g_in(2, j).wait_recv()
    prepare(2)
    hear(2)
    tell(3)
    relay(2, 1)
    relay(1, 1)
    whole(0)
    multiply(0, first=True)
    for j in (1, 2, 3):
        g_in(3, j).wait_recv()
    prepare(3)
    relay(3, 0)
    whole(2)
    multiply(2)
    relay(3, 1)
    whole(1)
    multiply(1)
    whole(3)
    multiply(3, last=True)
    hear(3)

    def o_out(dz, sp):
        to = lax.rem(z + dz, NZ)
        half = lax.div(rho, 2)
        target = device(x, yl, core, to, sp * 2 + 1 - lax.rem(rho, 2))
        return remote(zsend.at[to, sp], zrecv.at[dz, half], z_s.at[dz, sp], z_r.at[dz, half], target)

    def o_in(dz, half):
        source = device(x, yl, core, lax.rem(z + NZ - dz, NZ), half * 2 + 1 - lax.rem(rho, 2))
        piece = zrecv.at[dz, half]
        return remote(piece, piece, z_s.at[dz, half], z_r.at[dz, half], source)

    for dz in (4, 3, 5, 2, 6, 1, 7, 0):
        for sp in range(2):
            o_out(dz, sp).start()

    for e in range(NH):
        a_out(e).wait_send()
        for o in range(2):
            for dx in range(1, NX):
                x_out(dx, e, o).wait_send()
            for dx in range(NX):
                s_copy(dx, e, o, core).wait_send()
        y_out(e).wait_send()
        z_out(e).wait_send()
        if e != 2:
            f_out(e).wait_send()
    d_out().wait_send()

    totals = [None, None]
    for dz in (0, 1, 7, 2, 6, 3, 5, 4):
        for half in range(2):
            o_in(dz, half).wait_recv()
            piece = zrecv[dz, half].astype(F32)
            totals[dz % 2] = piece if totals[dz % 2] is None else totals[dz % 2] + piece
    for odd in range(2):
        first = lax.rem(z + odd, 2) * 2
        for c in range(2):
            out_ref[first + c] = totals[odd][16 * c:16 * c + 16]
    for dz in range(NZ):
        for sp in range(2):
            o_out(dz, sp).wait_send()


def shards(modes, momenta):
    dma = pltpu.SemaphoreType.DMA
    return pl.pallas_call(
        kernel,
        out_shape=jax.ShapeDtypeStruct((4, 16, 256), F32),
        in_specs=[
            pl.BlockSpec(memory_space=pl.ANY),
            pl.BlockSpec(memory_space=pl.ANY),
        ],
        out_specs=pl.BlockSpec(memory_space=pltpu.VMEM),
        scratch_shapes=[
            pltpu.VMEM((2, 1, 12, 16, 128), BF16),
            pltpu.SMEM((4, 3), jnp.int32),
            pltpu.VMEM((NH, 64, KEY), BF16),
            pltpu.VMEM((NH, 16, 16, KEY), BF16),
            pltpu.VMEM((NH, 512, KEY), BF16),
            pltpu.VMEM((NH, 512, KEY), BF16),
            pltpu.VMEM((512, 256), F32),
            pltpu.VMEM((2, 32, 128), F32),
            pltpu.VMEM((NZ, 2, 32, 256), BF16),
            pltpu.VMEM((NZ, 2, 32, 256), BF16),
            pltpu.SemaphoreType.REGULAR((4, 2)),
            dma((2,)),
            dma((4, 4)), dma((3, 4)),
            dma((NH,)), dma((NH,)),
            dma((NX - 1, NH, 2)), dma((NX - 1, NH, 2)),
            dma((NX, NH, 2)), dma((NX, NH, 2)),
            dma((NZ, 2)), dma((NZ, 2)),
        ],
        compiler_params=pltpu.CompilerParams(
            collective_id=0, has_side_effects=True, vmem_limit_bytes=56 * 1024 * 1024
        ),
    )(jnp.transpose(modes, (0, 1, 3, 2, 4)), momenta)


def solution(mesh):
    placed = (P(None, None, "blk", None, "site"), P())
    return jax.shard_map(
        shards, mesh=mesh, in_specs=placed, out_specs=P("site", "blk", None), check_vma=False
    )
```

```python
import math

import jax
import jax.numpy as jnp
from jax import lax
from jax.experimental import pallas as pl
from jax.experimental.pallas import tpu as pltpu
from jax.sharding import PartitionSpec as P

LEXT = 48
TWO_PI = 2.0 * math.pi
MESH = pl.DeviceIdType.MESH
F32 = jnp.float32
BF16 = jnp.bfloat16

NX, NZ, NH = 4, 8, 4
FAR = (0, 1, 3, 2)
SLOT = tuple(FAR.index(far) for far in range(NX))
KEY = 768
ROWS = (((1,), (1,)), ((), ()))


def remote(src, dst, send_sem, recv_sem, target):
    return pltpu.make_async_remote_copy(
        src_ref=src, dst_ref=dst, send_sem=send_sem, recv_sem=recv_sem,
        device_id=target, device_id_type=MESH,
    )


def flip(place):
    return place + 1 - 2 * lax.rem(place, 2)


def spin_rows(spin):
    return pl.ds(pl.multiple_of(spin * 16, 16), 16)


def kernel(
    modes_ref, mom_ref, out_ref,
    stage, mom, rows, cols, left, acc, acc_far, wave, near_out, near_in, far_out, far_in, tiles,
    hand, in_s, g_s, g_r, a_s, a_r, x_s, x_r, w_s, w_r, s_s, s_r, o_s, o_r,
):
    blk = lax.axis_index("blk")
    site = lax.axis_index("site")
    x = lax.div(blk, 4)
    yl = lax.rem(lax.div(blk, 2), 2)
    core = lax.rem(blk, 2)
    z = lax.div(site, 4)
    rho = lax.rem(site, 4)

    ahead = lax.rem(rho + 1 + 2 * yl, NH)
    behind = lax.rem(rho + 3 - 2 * yl, NH)

    def z_of(e):
        return flip(z) if e // 2 else z

    def spin_of(e):
        hi = lax.rem(rho + e, 2)
        return (1 - hi) * 2 + lax.rem(z_of(e), 2)

    spin = spin_of(0)

    def device(x, yl, core, z, hi):
        return (x * 4 + yl * 2 + core, z * 4 + hi)

    def lane_of(o):
        return yl if o == 0 else 1 - yl

    barrier = pltpu.get_barrier_semaphore()
    partners = [device(x, yl, 1 - core, z, rho)]
    partners += [device(lax.rem(x + dx, NX), yl, core, z, rho) for dx in (1, NX - 1)]
    partners += [device(x, 1 - yl, core, z_of(e), ahead if e % 2 else rho) for e in range(NH)]
    partners += [device(x, yl, core, flip(z), hi) for hi in (ahead, behind)]
    along_z = [device(x, yl, core, lax.rem(z + dz, NZ), rho) for dz in (2, NZ - 2, 1, NZ - 1)]
    along_y = [device(x, yl, core, z, lax.rem(rho + dh, NH)) for dh in (1, NH - 1)]
    partners += along_z + along_y
    for target in partners:
        pl.semaphore_signal(barrier, inc=1, device_id=target, device_id_type=MESH)
    get_modes = pltpu.make_async_copy(modes_ref, stage, in_s.at[0])
    get_modes.start()
    get_mom = pltpu.make_async_copy(mom_ref, mom, in_s.at[1])
    get_mom.start()

    get_modes.wait()
    for c in range(2):
        for s in range(4):
            for a in range(3):
                rows[0, pl.ds(16 * s, 16), pl.ds((c * 3 + a) * 128, 128)] = stage[c, 0, 3 * s + a]

    def gather(e, spin_e, e_from, to, way=0):
        return remote(
            rows.at[e_from, spin_rows(spin_e), :], rows.at[e, spin_rows(spin_e), :],
            g_s.at[e - 1 + way, spin_e], g_r.at[e - 1, spin_e], to,
        )

    def y_out(j):
        return gather(1, spin_of(j), 0, device(x, yl, core, z, behind))

    def z_out(j):
        return gather(2, spin_of(j), 0, device(x, yl, core, flip(z), rho))

    def d_out():
        return gather(3, spin_of(3), 0, device(x, yl, core, flip(z), behind), 1)

    def f_out(j):
        return gather(3, spin_of(j), 1, device(x, yl, core, flip(z), rho))

    def g_in(e, j):
        to = device(x, yl, core, flip(z), rho) if e > 1 else device(x, yl, core, z, ahead)
        return gather(e, spin_of(j), e, to)

    def piece(e, far, o, side):
        return cols.at[e, SLOT[far % NX], 0, lane_of(o), side]

    def a_out(e):
        to = device(x, 1 - yl, core, z_of(e), ahead if e % 2 else rho)
        return remote(rows.at[0, spin_rows(spin_of(e)), :], piece(e, 0, 0, core), a_s.at[e], a_r.at[e], to)

    def a_in(e):
        into = piece(e, 0, 1, core)
        return remote(into, into, a_s.at[e], a_r.at[e], device(x, 1 - yl, core, z_of(e), ahead if e % 2 else rho))

    def along_x(dx):
        return device(lax.rem(x + dx + NX, NX), yl, core, z, rho)

    def x_out(dx, e, o):
        at = (dx + 1) // 2
        return remote(
            piece(e, 0, o, core), piece(e, -dx, o, core), x_s.at[at, e, o], x_r.at[at, e, o], along_x(dx)
        )

    def x_in(dx, e, o):
        at, into = (dx + 1) // 2, piece(e, -dx, o, core)
        return remote(into, into, x_s.at[at, e, o], x_r.at[at, e, o], along_x(dx))

    def w_out(e, o):
        dx = 1 - 2 * o
        return remote(piece(e, -dx, o, core), piece(e, 2, o, core), w_s.at[e, o], w_r.at[e, o], along_x(dx))

    def w_in(e, o):
        into = piece(e, 2, o, core)
        return remote(into, into, w_s.at[e, o], w_r.at[e, o], along_x(1 - 2 * o))

    def s_copy(far, e, o, side):
        at = SLOT[far % NX]
        both = piece(e, far, o, side)
        return remote(both, both, s_s.at[at, e, o], s_r.at[at, e, o], device(x, yl, 1 - core, z, rho))

    def spread(e, o):
        if o == 0:
            cols[e, 0, 0, yl, core] = rows[e, spin_rows(spin), :]
        x_out(1, e, o).start()
        x_out(-1, e, o).start()
        s_copy(0, e, o, core).start()

    def relay(e, o):
        x_in(1, e, o).wait_recv()
        x_in(-1, e, o).wait_recv()
        w_out(e, o).start()
        s_copy(1, e, o, core).start()
        s_copy(-1, e, o, core).start()

    def relay_far(e, o):
        w_in(e, o).wait_recv()
        s_copy(2, e, o, core).start()

    def whole(e, far):
        for o in range(2):
            s_copy(far, e, o, 1 - core).wait_recv()
        at = SLOT[far % NX]
        for l in range(2):
            for side in range(2):
                for a in range(3):
                    cols[e, at, 1, l, side, :, pl.ds(a * 128, 128)] = cols[e, at, 0, l, side, :, pl.ds((3 + a) * 128, 128)]
                    cols[e, at, 1, l, side, :, pl.ds((3 + a) * 128, 128)] = -cols[e, at, 0, l, side, :, pl.ds(a * 128, 128)]

    def prepare(e):
        for k in range(4):
            cos = wave[0, pl.ds(8 * k + e, 1), :]
            sin = wave[1, pl.ds(8 * k + e, 1), :]
            for s in range(4):
                for a in range(3):
                    ur = rows[e, pl.ds(16 * s, 16), pl.ds(a * 128, 128)].astype(F32)
                    ui = rows[e, pl.ds(16 * s, 16), pl.ds((3 + a) * 128, 128)].astype(F32)
                    for c, value in enumerate((ur * cos - ui * sin, ui * cos + ur * sin)):
                        high = value.astype(BF16)
                        at, lanes = k * 64 + s * 16, pl.ds((3 * c + a) * 128, 128)
                        left[e, pl.ds(at, 16), lanes] = high
                        left[e, pl.ds(256 + at, 16), lanes] = (value - high.astype(F32)).astype(BF16)

    def product(e, right):
        part = lax.dot_general(left[e], right, ROWS, preferred_element_type=F32)
        return part[:256] + part[256:]

    def put(out, sums, slots):
        for k in range(4):
            for s in range(4):
                for slot in range(slots):
                    tile = sums[64 * k + 16 * s:64 * k + 16 * s + 16, 128 * slot:128 * slot + 128]
                    out[2 * k + s // 2, s % 2, slot] = tile.astype(BF16)

    def multiply_near(e, first=False, last=False):
        part = product(e, cols[e, pl.ds(0, 3)].reshape(384, KEY))
        if not first:
            part += acc[...]
        if last:
            put(near_out, part, 3)
        else:
            acc[...] = part

    def multiply_far(es, first=False, last=False):
        part = None if first else acc_far[...]
        for e in es:
            more = product(e, cols[e, 3].reshape(128, KEY))
            part = more if part is None else part + more
        if last:
            put(far_out, part, 1)
        else:
            acc_far[...] = part

    def tell(turn):
        for side, to in enumerate(along_y if turn else along_z[:2]):
            pl.semaphore_signal(hand.at[turn, side], inc=1, device_id=to, device_id_type=MESH)

    def hear(turn):
        for side in range(2):
            pl.semaphore_wait(hand.at[turn, side], 1)

    def o_out(part, dz, sp):
        to = lax.rem(z + dz, NZ)
        half = lax.div(rho, 2)
        target = device(x, yl, core, to, sp * 2 + 1 - lax.rem(rho, 2))
        src, dst = ((near_out, near_in), (far_out, far_in))[part]
        return remote(src.at[to, sp], dst.at[dz, half], o_s.at[part, dz, sp], o_r.at[part, dz, half], target)

    def o_in(part, dz, half):
        source = device(x, yl, core, lax.rem(z + NZ - dz, NZ), half * 2 + 1 - lax.rem(rho, 2))
        into = (near_in, far_in)[part].at[dz, half]
        return remote(into, into, o_s.at[part, dz, half], o_r.at[part, dz, half], source)

    def scatter(part):
        for dz in (4, 3, 5, 2, 6, 1, 7, 0):
            for sp in range(2):
                o_out(part, dz, sp).start()

    pl.semaphore_wait(barrier, len(partners))
    y_out(1).start()
    z_out(2).start()
    a_out(0).start()
    spread(0, 0)
    d_out().start()
    a_out(3).start()
    a_out(1).start()
    a_out(2).start()
    tell(0)

    get_mom.wait()
    row = lax.broadcasted_iota(jnp.int32, (8, 128), 0)
    lane = lax.broadcasted_iota(jnp.int32, (8, 128), 1)
    hi_row = rho + (row & 1) * (ahead - rho)
    z_row = z + (lax.shift_right_logical(row, 1) & 1) * (flip(z) - z)
    flat = ((z_row * 4 + hi_row) * 128 + lane).astype(F32)
    plane = jnp.floor((flat + 0.5) * (1.0 / (LEXT * LEXT)))
    line = jnp.floor((flat + 0.5) * (1.0 / LEXT))
    coords = (flat - LEXT * line, line - LEXT * plane, plane)
    for k in range(4):
        turns = sum(mom[k, d].astype(F32) * coords[d] for d in range(3))
        turns = turns - LEXT * jnp.floor((turns + 0.5) * (1.0 / LEXT))
        angle = turns * (TWO_PI / LEXT)
        wave[0, pl.ds(8 * k, 8), :] = jnp.cos(angle)
        wave[1, pl.ds(8 * k, 8), :] = jnp.sin(angle)

    prepare(0)
    a_in(0).wait_recv()
    spread(0, 1)
    g_in(2, 0).wait_recv()
    spread(2, 0)
    g_in(1, 0).wait_recv()
    spread(1, 0)
    f_out(0).start()
    y_out(0).start()
    z_out(0).start()
    y_out(2).start()
    z_out(1).start()
    y_out(3).start()
    z_out(3).start()
    a_in(2).wait_recv()
    spread(2, 1)
    relay(0, 0)
    a_in(1).wait_recv()
    spread(1, 1)
    g_in(3, 0).wait_recv()
    spread(3, 0)
    a_in(3).wait_recv()
    spread(3, 1)
    relay(0, 1)
    relay(2, 0)
    g_in(1, 1).wait_recv()
    f_out(1).start()
    relay(1, 0)
    relay(2, 1)
    g_in(1, 3).wait_recv()
    f_out(3).start()
    hear(0)
    tell(1)
    relay(1, 1)
    relay(3, 0)
    relay(3, 1)
    for j in (1, 2, 3):
        g_in(2, j).wait_recv()
    prepare(2)
    relay_far(0, 0)
    relay_far(0, 1)
    g_in(1, 2).wait_recv()
    prepare(1)
    for far in (0, 1, -1):
        whole(0, far)
    multiply_near(0, first=True)
    relay_far(2, 0)
    relay_far(1, 0)
    for far in (0, 1, -1):
        whole(2, far)
    multiply_near(2)
    relay_far(2, 1)
    relay_far(1, 1)
    for far in (0, 1, -1):
        whole(1, far)
    multiply_near(1)
    for j in (1, 2, 3):
        g_in(3, j).wait_recv()
    prepare(3)
    relay_far(3, 0)
    relay_far(3, 1)
    for far in (0, 1, -1):
        whole(3, far)
    multiply_near(3, last=True)
    hear(1)
    scatter(0)
    for e in (0, 2, 1):
        whole(e, 2)
    multiply_far((0, 2, 1), first=True)
    whole(3, 2)
    multiply_far((3,), last=True)
    scatter(1)

    for e in range(NH):
        a_out(e).wait_send()
        for o in range(2):
            x_out(1, e, o).wait_send()
            x_out(-1, e, o).wait_send()
            w_out(e, o).wait_send()
            for far in range(NX):
                s_copy(far, e, o, core).wait_send()
        y_out(e).wait_send()
        z_out(e).wait_send()
        if e != 2:
            f_out(e).wait_send()
    d_out().wait_send()

    for part, slots in ((0, 3), (1, 1)):
        totals = [None, None]
        for dz in (0, 1, 7, 2, 6, 3, 5, 4):
            for half in range(2):
                o_in(part, dz, half).wait_recv()
                some = (near_in, far_in)[part][dz, half].astype(F32)
                totals[dz % 2] = some if totals[dz % 2] is None else totals[dz % 2] + some
        for odd in range(2):
            for slot in range(slots):
                far = FAR[3 * part + slot]
                tiles[lax.rem(z + odd, 2), lax.rem(x + far, NX)] = totals[odd][slot]
    low = lax.broadcasted_iota(jnp.int32, (16, 128), 1) < 64
    for r in range(2):
        for v in range(2):
            even, odd = tiles[r, 2 * v], tiles[r, 2 * v + 1]
            out_ref[2 * r, :, pl.ds(128 * v, 128)] = jnp.where(low, even, pltpu.roll(odd, 64, 1))
            out_ref[2 * r + 1, :, pl.ds(128 * v, 128)] = jnp.where(low, pltpu.roll(even, 64, 1), odd)
    for part in range(2):
        for dz in range(NZ):
            for sp in range(2):
                o_out(part, dz, sp).wait_send()


def shards(modes, momenta):
    dma = pltpu.SemaphoreType.DMA
    return pl.pallas_call(
        kernel,
        out_shape=jax.ShapeDtypeStruct((4, 16, 256), F32),
        in_specs=[
            pl.BlockSpec(memory_space=pl.ANY),
            pl.BlockSpec(memory_space=pl.ANY),
        ],
        out_specs=pl.BlockSpec(memory_space=pltpu.VMEM),
        scratch_shapes=[
            pltpu.VMEM((2, 1, 12, 16, 128), BF16),
            pltpu.SMEM((4, 3), jnp.int32),
            pltpu.VMEM((NH, 64, KEY), BF16),
            pltpu.VMEM((NH, NX, 2, 2, 2, 16, KEY), BF16),
            pltpu.VMEM((NH, 512, KEY), BF16),
            pltpu.VMEM((256, 384), F32),
            pltpu.VMEM((256, 128), F32),
            pltpu.VMEM((2, 32, 128), F32),
            pltpu.VMEM((NZ, 2, 3, 16, 128), BF16),
            pltpu.VMEM((NZ, 2, 3, 16, 128), BF16),
            pltpu.VMEM((NZ, 2, 1, 16, 128), BF16),
            pltpu.VMEM((NZ, 2, 1, 16, 128), BF16),
            pltpu.VMEM((2, NX, 16, 128), F32),
            pltpu.SemaphoreType.REGULAR((2, 2)),
            dma((2,)),
            dma((4, 4)), dma((3, 4)),
            dma((NH,)), dma((NH,)),
            dma((2, NH, 2)), dma((2, NH, 2)),
            dma((NH, 2)), dma((NH, 2)),
            dma((NX, NH, 2)), dma((NX, NH, 2)),
            dma((2, NZ, 2)), dma((2, NZ, 2)),
        ],
        compiler_params=pltpu.CompilerParams(
            collective_id=0, has_side_effects=True, vmem_limit_bytes=56 * 1024 * 1024
        ),
    )(jnp.transpose(modes, (0, 1, 3, 2, 4)), momenta)


def solution(mesh):
    placed = (P(None, None, "blk", None, "site"), P())
    return jax.shard_map(
        shards, mesh=mesh, in_specs=placed, out_specs=P("site", "blk", None), check_vma=False
    )
```

```python
import math

import jax
import jax.numpy as jnp
from jax import lax
from jax.experimental import pallas as pl
from jax.experimental.pallas import tpu as pltpu
from jax.sharding import PartitionSpec as P

LEXT = 48
TWO_PI = 2.0 * math.pi
MESH = pl.DeviceIdType.MESH
F32 = jnp.float32
BF16 = jnp.bfloat16

NX, NZ, NH = 4, 8, 4
FAR = (0, 1, 3, 2)
SLOT = tuple(FAR.index(far) for far in range(NX))
KEY = 768
ROWS = (((1,), (1,)), ((), ()))


def remote(src, dst, send_sem, recv_sem, target):
    return pltpu.make_async_remote_copy(
        src_ref=src, dst_ref=dst, send_sem=send_sem, recv_sem=recv_sem,
        device_id=target, device_id_type=MESH,
    )


def flip(place):
    return place + 1 - 2 * lax.rem(place, 2)


def spin_rows(spin):
    return pl.ds(pl.multiple_of(spin * 16, 16), 16)


def kernel(
    modes_ref, mom_ref, out_ref,
    stage, mom, rows, cols, left, acc, acc_far, wave, near_out, near_in, far_out, far_in, tiles,
    hand, in_s, g_s, g_r, a_s, a_r, x_s, x_r, w_s, w_r, s_s, s_r, o_s, o_r,
):
    blk = lax.axis_index("blk")
    site = lax.axis_index("site")
    x = lax.div(blk, 4)
    yl = lax.rem(lax.div(blk, 2), 2)
    core = lax.rem(blk, 2)
    z = lax.div(site, 4)
    rho = lax.rem(site, 4)

    ahead = lax.rem(rho + 3 + 2 * yl, NH)
    behind = lax.rem(rho + 1 + 2 * yl, NH)

    def z_of(e):
        return flip(z) if e // 2 else z

    def spin_of(e):
        hi = lax.rem(rho + e, 2)
        return (1 - hi) * 2 + lax.rem(z_of(e), 2)

    spin = spin_of(0)

    def device(x, yl, core, z, hi):
        return (x * 4 + yl * 2 + core, z * 4 + hi)

    def lane_of(o):
        return yl if o == 0 else 1 - yl

    barrier = pltpu.get_barrier_semaphore()
    partners = [device(x, yl, 1 - core, z, rho)]
    partners += [device(lax.rem(x + dx, NX), yl, core, z, rho) for dx in (1, NX - 1)]
    partners += [device(x, 1 - yl, core, z_of(e), ahead if e % 2 else rho) for e in range(NH)]
    partners += [device(x, yl, core, flip(z), hi) for hi in (ahead, behind)]
    along_z = [device(x, yl, core, lax.rem(z + dz, NZ), rho) for dz in (2, NZ - 2, 1, NZ - 1)]
    along_y = [device(x, yl, core, z, lax.rem(rho + dh, NH)) for dh in (1, NH - 1)]
    partners += along_z + along_y
    for target in partners:
        pl.semaphore_signal(barrier, inc=1, device_id=target, device_id_type=MESH)
    get_modes = pltpu.make_async_copy(modes_ref, stage, in_s.at[0])
    get_modes.start()
    get_mom = pltpu.make_async_copy(mom_ref, mom, in_s.at[1])
    get_mom.start()

    get_modes.wait()
    for c in range(2):
        for s in range(4):
            for a in range(3):
                rows[0, pl.ds(16 * s, 16), pl.ds((c * 3 + a) * 128, 128)] = stage[c, 0, 3 * s + a]

    def gather(e, spin_e, e_from, to):
        return remote(
            rows.at[e_from, spin_rows(spin_e), :], rows.at[e, spin_rows(spin_e), :],
            g_s.at[e - 1, spin_e], g_r.at[e - 1, spin_e], to,
        )

    def y_out(j):
        return gather(1, spin_of(j), 0, device(x, yl, core, z, behind))

    def z_out(j):
        return gather(2, spin_of(j), 0, device(x, yl, core, flip(z), rho))

    def d_out(j):
        return gather(3, spin_of(j), 0, device(x, yl, core, flip(z), behind))

    def g_in(e, j):
        to = device(x, yl, core, flip(z), rho) if e > 1 else device(x, yl, core, z, ahead)
        return gather(e, spin_of(j), e, to)

    def piece(e, far, o, side):
        return cols.at[e, SLOT[far % NX], 0, lane_of(o), side]

    def a_out(e):
        to = device(x, 1 - yl, core, z_of(e), ahead if e % 2 else rho)
        return remote(rows.at[0, spin_rows(spin_of(e)), :], piece(e, 0, 0, core), a_s.at[e], a_r.at[e], to)

    def a_in(e):
        into = piece(e, 0, 1, core)
        return remote(into, into, a_s.at[e], a_r.at[e], device(x, 1 - yl, core, z_of(e), ahead if e % 2 else rho))

    def along_x(dx):
        return device(lax.rem(x + dx + NX, NX), yl, core, z, rho)

    def x_out(dx, e, o):
        at = (dx + 1) // 2
        return remote(
            piece(e, 0, o, core), piece(e, -dx, o, core), x_s.at[at, e, o], x_r.at[at, e, o], along_x(dx)
        )

    def x_in(dx, e, o):
        at, into = (dx + 1) // 2, piece(e, -dx, o, core)
        return remote(into, into, x_s.at[at, e, o], x_r.at[at, e, o], along_x(dx))

    def w_out(e, o):
        dx = 1 - 2 * o
        return remote(piece(e, -dx, o, core), piece(e, 2, o, core), w_s.at[e, o], w_r.at[e, o], along_x(dx))

    def w_in(e, o):
        into = piece(e, 2, o, core)
        return remote(into, into, w_s.at[e, o], w_r.at[e, o], along_x(1 - 2 * o))

    def s_copy(far, e, side):
        at = SLOT[far % NX]
        both = cols.at[e, at, 0, :, side]
        return remote(both, both, s_s.at[at, e], s_r.at[at, e], device(x, yl, 1 - core, z, rho))

    def spread(e, o):
        if o == 0:
            cols[e, 0, 0, yl, core] = rows[e, spin_rows(spin), :]
        x_out(1, e, o).start()
        x_out(-1, e, o).start()

    def relay(e, o):
        x_in(1, e, o).wait_recv()
        x_in(-1, e, o).wait_recv()
        w_out(e, o).start()

    def relay_far(e, o):
        w_in(e, o).wait_recv()

    def whole(e, far):
        s_copy(far, e, 1 - core).wait_recv()
        at = SLOT[far % NX]
        for l in range(2):
            for side in range(2):
                for a in range(3):
                    cols[e, at, 1, l, side, :, pl.ds(a * 128, 128)] = cols[e, at, 0, l, side, :, pl.ds((3 + a) * 128, 128)]
                    cols[e, at, 1, l, side, :, pl.ds((3 + a) * 128, 128)] = -cols[e, at, 0, l, side, :, pl.ds(a * 128, 128)]

    def prepare(e):
        for k in range(4):
            cos = wave[0, pl.ds(8 * k + e, 1), :]
            sin = wave[1, pl.ds(8 * k + e, 1), :]
            for s in range(4):
                for a in range(3):
                    ur = rows[e, pl.ds(16 * s, 16), pl.ds(a * 128, 128)].astype(F32)
                    ui = rows[e, pl.ds(16 * s, 16), pl.ds((3 + a) * 128, 128)].astype(F32)
                    for c, value in enumerate((ur * cos - ui * sin, ui * cos + ur * sin)):
                        high = value.astype(BF16)
                        at, lanes = k * 64 + s * 16, pl.ds((3 * c + a) * 128, 128)
                        left[e, pl.ds(at, 16), lanes] = high
                        left[e, pl.ds(256 + at, 16), lanes] = (value - high.astype(F32)).astype(BF16)

    def product(e, right):
        part = lax.dot_general(left[e], right, ROWS, preferred_element_type=F32)
        return part[:256] + part[256:]

    def put(out, sums, slots):
        for k in range(4):
            for s in range(4):
                for slot in range(slots):
                    tile = sums[64 * k + 16 * s:64 * k + 16 * s + 16, 128 * slot:128 * slot + 128]
                    out[2 * k + s // 2, s % 2, slot] = tile.astype(BF16)

    def multiply_near(e, first=False, last=False):
        part = product(e, cols[e, pl.ds(0, 3)].reshape(384, KEY))
        if not first:
            part += acc[...]
        if last:
            put(near_out, part, 3)
        else:
            acc[...] = part

    def multiply_far(es, first=False, last=False):
        part = None if first else acc_far[...]
        for e in es:
            more = product(e, cols[e, 3].reshape(128, KEY))
            part = more if part is None else part + more
        if last:
            put(far_out, part, 1)
        else:
            acc_far[...] = part

    def tell(turn):
        for side, to in enumerate(along_y if turn else along_z[:2]):
            pl.semaphore_signal(hand.at[turn, side], inc=1, device_id=to, device_id_type=MESH)

    def hear(turn):
        for side in range(2):
            pl.semaphore_wait(hand.at[turn, side], 1)

    def o_out(part, dz, sp):
        to = lax.rem(z + dz, NZ)
        half = lax.div(rho, 2)
        target = device(x, yl, core, to, sp * 2 + 1 - lax.rem(rho, 2))
        src, dst = ((near_out, near_in), (far_out, far_in))[part]
        return remote(src.at[to, sp], dst.at[dz, half], o_s.at[part, dz, sp], o_r.at[part, dz, half], target)

    def o_in(part, dz, half):
        source = device(x, yl, core, lax.rem(z + NZ - dz, NZ), half * 2 + 1 - lax.rem(rho, 2))
        into = (near_in, far_in)[part].at[dz, half]
        return remote(into, into, o_s.at[part, dz, half], o_r.at[part, dz, half], source)

    def scatter(part):
        for dz in (4, 3, 5, 2, 6, 1, 7, 0):
            for sp in range(2):
                o_out(part, dz, sp).start()

    pl.semaphore_wait(barrier, len(partners))
    y_out(1).start()
    z_out(2).start()
    a_out(0).start()
    spread(0, 0)
    d_out(3).start()
    a_out(3).start()
    a_out(1).start()
    a_out(2).start()
    tell(0)

    get_mom.wait()
    row = lax.broadcasted_iota(jnp.int32, (8, 128), 0)
    lane = lax.broadcasted_iota(jnp.int32, (8, 128), 1)
    hi_row = rho + (row & 1) * (ahead - rho)
    z_row = z + (lax.shift_right_logical(row, 1) & 1) * (flip(z) - z)
    flat = ((z_row * 4 + hi_row) * 128 + lane).astype(F32)
    plane = jnp.floor((flat + 0.5) * (1.0 / (LEXT * LEXT)))
    line = jnp.floor((flat + 0.5) * (1.0 / LEXT))
    coords = (flat - LEXT * line, line - LEXT * plane, plane)
    for k in range(4):
        turns = sum(mom[k, d].astype(F32) * coords[d] for d in range(3))
        turns = turns - LEXT * jnp.floor((turns + 0.5) * (1.0 / LEXT))
        angle = turns * (TWO_PI / LEXT)
        wave[0, pl.ds(8 * k, 8), :] = jnp.cos(angle)
        wave[1, pl.ds(8 * k, 8), :] = jnp.sin(angle)

    def share(e):
        for far in (1, -1):
            s_copy(far, e, core).start()

    prepare(0)
    a_in(0).wait_recv()
    spread(0, 1)
    g_in(2, 0).wait_recv()
    spread(2, 0)
    g_in(1, 0).wait_recv()
    spread(1, 0)
    for j, i in ((0, 0), (2, 1), (3, 3)):
        z_out(i).start()
        y_out(j).start()
        d_out(j if j < 3 else 1).start()
    s_copy(0, 0, core).start()
    a_in(2).wait_recv()
    spread(2, 1)
    relay(0, 0)
    a_in(1).wait_recv()
    spread(1, 1)
    g_in(3, 0).wait_recv()
    spread(3, 0)
    a_in(3).wait_recv()
    spread(3, 1)
    for e in (2, 1, 3):
        s_copy(0, e, core).start()
    relay(0, 1)
    share(0)
    relay(2, 0)
    relay(1, 0)
    relay(2, 1)
    share(2)
    hear(0)
    tell(1)
    relay(1, 1)
    share(1)
    relay(3, 0)
    relay(3, 1)
    share(3)
    def far_of(e):
        relay_far(e, 0)
        relay_far(e, 1)
        s_copy(2, e, core).start()

    for j in (1, 2, 3):
        g_in(2, j).wait_recv()
    prepare(2)
    far_of(0)
    for far in (0, 1, -1):
        whole(0, far)
    multiply_near(0, first=True)
    for j in (1, 2, 3):
        g_in(1, j).wait_recv()
    prepare(1)
    far_of(2)
    for far in (0, 1, -1):
        whole(2, far)
    multiply_near(2)
    far_of(1)
    for far in (0, 1, -1):
        whole(1, far)
    multiply_near(1)
    for j in (1, 2, 3):
        g_in(3, j).wait_recv()
    prepare(3)
    far_of(3)
    for far in (0, 1, -1):
        whole(3, far)
    multiply_near(3, last=True)
    hear(1)
    scatter(0)
    for e in (0, 2, 1):
        whole(e, 2)
    multiply_far((0, 2, 1), first=True)
    whole(3, 2)
    multiply_far((3,), last=True)
    scatter(1)

    for e in range(NH):
        a_out(e).wait_send()
        for o in range(2):
            x_out(1, e, o).wait_send()
            x_out(-1, e, o).wait_send()
            w_out(e, o).wait_send()
        for far in range(NX):
            s_copy(far, e, core).wait_send()
        y_out(e).wait_send()
        z_out(e).wait_send()
        d_out(e).wait_send()

    for part in range(2):
        for dz in range(NZ):
            for sp in range(2):
                o_out(part, dz, sp).wait_send()

    for part, slots in ((0, 3), (1, 1)):
        totals = [None, None]
        for dz in (0, 1, 7, 2, 6, 3, 5, 4):
            for half in range(2):
                o_in(part, dz, half).wait_recv()
                some = (near_in, far_in)[part][dz, half].astype(F32)
                totals[dz % 2] = some if totals[dz % 2] is None else totals[dz % 2] + some
        for odd in range(2):
            for slot in range(slots):
                far = FAR[3 * part + slot]
                tiles[lax.rem(z + odd, 2), lax.rem(x + far, NX)] = totals[odd][slot]
    low = lax.broadcasted_iota(jnp.int32, (16, 128), 1) < 64
    for r in range(2):
        for v in range(2):
            even, odd = tiles[r, 2 * v], tiles[r, 2 * v + 1]
            out_ref[2 * r, :, pl.ds(128 * v, 128)] = jnp.where(low, even, pltpu.roll(odd, 64, 1))
            out_ref[2 * r + 1, :, pl.ds(128 * v, 128)] = jnp.where(low, pltpu.roll(even, 64, 1), odd)


def shards(modes, momenta):
    dma = pltpu.SemaphoreType.DMA
    return pl.pallas_call(
        kernel,
        out_shape=jax.ShapeDtypeStruct((4, 16, 256), F32),
        in_specs=[
            pl.BlockSpec(memory_space=pl.ANY),
            pl.BlockSpec(memory_space=pl.ANY),
        ],
        out_specs=pl.BlockSpec(memory_space=pltpu.VMEM),
        scratch_shapes=[
            pltpu.VMEM((2, 1, 12, 16, 128), BF16),
            pltpu.SMEM((4, 3), jnp.int32),
            pltpu.VMEM((NH, 64, KEY), BF16),
            pltpu.VMEM((NH, NX, 2, 2, 2, 16, KEY), BF16),
            pltpu.VMEM((NH, 512, KEY), BF16),
            pltpu.VMEM((256, 384), F32),
            pltpu.VMEM((256, 128), F32),
            pltpu.VMEM((2, 32, 128), F32),
            pltpu.VMEM((NZ, 2, 3, 16, 128), BF16),
            pltpu.VMEM((NZ, 2, 3, 16, 128), BF16),
            pltpu.VMEM((NZ, 2, 1, 16, 128), BF16),
            pltpu.VMEM((NZ, 2, 1, 16, 128), BF16),
            pltpu.VMEM((2, NX, 16, 128), F32),
            pltpu.SemaphoreType.REGULAR((2, 2)),
            dma((2,)),
            dma((3, 4)), dma((3, 4)),
            dma((NH,)), dma((NH,)),
            dma((2, NH, 2)), dma((2, NH, 2)),
            dma((NH, 2)), dma((NH, 2)),
            dma((NX, NH)), dma((NX, NH)),
            dma((2, NZ, 2)), dma((2, NZ, 2)),
        ],
        compiler_params=pltpu.CompilerParams(
            collective_id=0, has_side_effects=True, vmem_limit_bytes=56 * 1024 * 1024
        ),
    )(jnp.transpose(modes, (0, 1, 3, 2, 4)), momenta)


def solution(mesh):
    placed = (P(None, None, "blk", None, "site"), P())
    return jax.shard_map(
        shards, mesh=mesh, in_specs=placed, out_specs=P("site", "blk", None), check_vma=False
    )
```

```python
import math

import jax
import jax.numpy as jnp
from jax import lax
from jax.experimental import pallas as pl
from jax.experimental.pallas import tpu as pltpu
from jax.sharding import PartitionSpec as P

LEXT = 48
TWO_PI = 2.0 * math.pi
MESH = pl.DeviceIdType.MESH
F32 = jnp.float32
BF16 = jnp.bfloat16

NX, NZ, NH = 4, 8, 4
FAR = (0, 1, 3, 2)
SLOT = tuple(FAR.index(far) for far in range(NX))
KEY = 768
ROWS = (((1,), (1,)), ((), ()))


def remote(src, dst, send_sem, recv_sem, target):
    return pltpu.make_async_remote_copy(
        src_ref=src, dst_ref=dst, send_sem=send_sem, recv_sem=recv_sem,
        device_id=target, device_id_type=MESH,
    )


def flip(place):
    return place + 1 - 2 * lax.rem(place, 2)


def spin_rows(spin):
    return pl.ds(pl.multiple_of(spin * 16, 16), 16)


def kernel(
    modes_ref, mom_ref, out_ref,
    stage, mom, rows, cols, left, acc, acc_far, wave, near_out, near_in, far_out, far_in, tiles,
    hand, in_s, g_s, g_r, a_s, a_r, x_s, x_r, w_s, w_r, s_s, s_r, o_s, o_r,
):
    blk = lax.axis_index("blk")
    site = lax.axis_index("site")
    x = lax.div(blk, 4)
    yl = lax.rem(lax.div(blk, 2), 2)
    core = lax.rem(blk, 2)
    z = lax.div(site, 4)
    rho = lax.rem(site, 4)

    ahead = lax.rem(rho + 3 + 2 * yl, NH)
    behind = lax.rem(rho + 1 + 2 * yl, NH)

    def z_of(e):
        return flip(z) if e // 2 else z

    def spin_of(e):
        hi = lax.rem(rho + e, 2)
        return (1 - hi) * 2 + lax.rem(z_of(e), 2)

    spin = spin_of(0)

    def device(x, yl, core, z, hi):
        return (x * 4 + yl * 2 + core, z * 4 + hi)

    def lane_of(o):
        return yl if o == 0 else 1 - yl

    barrier = pltpu.get_barrier_semaphore()
    partners = [device(x, yl, 1 - core, z, rho)]
    partners += [device(lax.rem(x + dx, NX), yl, core, z, rho) for dx in (1, NX - 1)]
    partners += [device(x, 1 - yl, core, z_of(e), ahead if e % 2 else rho) for e in range(NH)]
    partners += [device(x, yl, core, flip(z), hi) for hi in (ahead, behind)]
    along_z = [device(x, yl, core, lax.rem(z + dz, NZ), rho) for dz in (2, NZ - 2, 1, NZ - 1)]
    along_y = [device(x, yl, core, z, lax.rem(rho + dh, NH)) for dh in (1, NH - 1)]
    partners += along_z + along_y
    for target in partners:
        pl.semaphore_signal(barrier, inc=1, device_id=target, device_id_type=MESH)
    get_modes = pltpu.make_async_copy(modes_ref, stage, in_s.at[0])
    get_modes.start()
    get_mom = pltpu.make_async_copy(mom_ref, mom, in_s.at[1])
    get_mom.start()

    get_modes.wait()
    for c in range(2):
        for s in range(4):
            for a in range(3):
                rows[0, pl.ds(16 * s, 16), pl.ds((c * 3 + a) * 128, 128)] = stage[c, 0, 3 * s + a]

    def gather(e, spin_e, e_from, to):
        return remote(
            rows.at[e_from, spin_rows(spin_e), :], rows.at[e, spin_rows(spin_e), :],
            g_s.at[e - 1, spin_e], g_r.at[e - 1, spin_e], to,
        )

    def y_out(j):
        return gather(1, spin_of(j), 0, device(x, yl, core, z, behind))

    def z_out(j):
        return gather(2, spin_of(j), 0, device(x, yl, core, flip(z), rho))

    def d_out(j):
        return gather(3, spin_of(j), 0, device(x, yl, core, flip(z), behind))

    def g_in(e, j):
        to = device(x, yl, core, flip(z), rho) if e > 1 else device(x, yl, core, z, ahead)
        return gather(e, spin_of(j), e, to)

    def piece(e, far, o, side):
        return cols.at[e, SLOT[far % NX], 0, lane_of(o), side]

    def a_out(e):
        to = device(x, 1 - yl, core, z_of(e), ahead if e % 2 else rho)
        return remote(rows.at[0, spin_rows(spin_of(e)), :], piece(e, 0, 0, core), a_s.at[e], a_r.at[e], to)

    def a_in(e):
        into = piece(e, 0, 1, core)
        return remote(into, into, a_s.at[e], a_r.at[e], device(x, 1 - yl, core, z_of(e), ahead if e % 2 else rho))

    def along_x(dx):
        return device(lax.rem(x + dx + NX, NX), yl, core, z, rho)

    def x_out(dx, e, o):
        at = (dx + 1) // 2
        return remote(
            piece(e, 0, o, core), piece(e, -dx, o, core), x_s.at[at, e, o], x_r.at[at, e, o], along_x(dx)
        )

    def x_in(dx, e, o):
        at, into = (dx + 1) // 2, piece(e, -dx, o, core)
        return remote(into, into, x_s.at[at, e, o], x_r.at[at, e, o], along_x(dx))

    def w_out(e, o):
        dx = 1 - 2 * o
        return remote(piece(e, -dx, o, core), piece(e, 2, o, core), w_s.at[e, o], w_r.at[e, o], along_x(dx))

    def w_in(e, o):
        into = piece(e, 2, o, core)
        return remote(into, into, w_s.at[e, o], w_r.at[e, o], along_x(1 - 2 * o))

    def s_copy(far, e, side):
        at = SLOT[far % NX]
        both = cols.at[e, at, 0, :, side]
        return remote(both, both, s_s.at[at, e], s_r.at[at, e], device(x, yl, 1 - core, z, rho))

    def spread(e, o):
        if o == 0:
            cols[e, 0, 0, yl, core] = rows[e, spin_rows(spin), :]
        x_out(1, e, o).start()
        x_out(-1, e, o).start()

    def relay(e, o):
        x_in(1, e, o).wait_recv()
        x_in(-1, e, o).wait_recv()
        w_out(e, o).start()

    def relay_far(e, o):
        w_in(e, o).wait_recv()

    def whole(e, far):
        s_copy(far, e, 1 - core).wait_recv()
        at = SLOT[far % NX]
        for l in range(2):
            for side in range(2):
                for a in range(3):
                    cols[e, at, 1, l, side, :, pl.ds(a * 128, 128)] = cols[e, at, 0, l, side, :, pl.ds((3 + a) * 128, 128)]
                    cols[e, at, 1, l, side, :, pl.ds((3 + a) * 128, 128)] = -cols[e, at, 0, l, side, :, pl.ds(a * 128, 128)]

    def prepare(e):
        for k in range(4):
            cos = wave[0, pl.ds(8 * k + e, 1), :]
            sin = wave[1, pl.ds(8 * k + e, 1), :]
            for s in range(4):
                for a in range(3):
                    ur = rows[e, pl.ds(16 * s, 16), pl.ds(a * 128, 128)].astype(F32)
                    ui = rows[e, pl.ds(16 * s, 16), pl.ds((3 + a) * 128, 128)].astype(F32)
                    for c, value in enumerate((ur * cos - ui * sin, ui * cos + ur * sin)):
                        high = value.astype(BF16)
                        at, lanes = k * 64 + s * 16, pl.ds((3 * c + a) * 128, 128)
                        left[e, pl.ds(at, 16), lanes] = high
                        left[e, pl.ds(256 + at, 16), lanes] = (value - high.astype(F32)).astype(BF16)

    def product(e, right):
        part = lax.dot_general(left[e], right, ROWS, preferred_element_type=F32)
        return part[:256] + part[256:]

    def put(out, sums, slots):
        for k in range(4):
            for s in range(4):
                for slot in range(slots):
                    tile = sums[64 * k + 16 * s:64 * k + 16 * s + 16, 128 * slot:128 * slot + 128]
                    out[2 * k + s // 2, s % 2, slot] = tile.astype(BF16)

    def multiply_near(e, first=False, last=False):
        part = product(e, cols[e, pl.ds(0, 3)].reshape(384, KEY))
        if not first:
            part += acc[...]
        if last:
            put(near_out, part, 3)
        else:
            acc[...] = part

    def multiply_far(es, first=False, last=False):
        part = None if first else acc_far[...]
        for e in es:
            more = product(e, cols[e, 3].reshape(128, KEY))
            part = more if part is None else part + more
        if last:
            put(far_out, part, 1)
        else:
            acc_far[...] = part

    def tell(turn):
        for side, to in enumerate(along_y if turn else along_z[:2]):
            pl.semaphore_signal(hand.at[turn, side], inc=1, device_id=to, device_id_type=MESH)

    def hear(turn):
        for side in range(2):
            pl.semaphore_wait(hand.at[turn, side], 1)

    def o_out(part, dz, sp):
        to = lax.rem(z + dz, NZ)
        half = lax.div(rho, 2)
        target = device(x, yl, core, to, sp * 2 + 1 - lax.rem(rho, 2))
        src, dst = ((near_out, near_in), (far_out, far_in))[part]
        return remote(src.at[to, sp], dst.at[dz, half], o_s.at[part, dz, sp], o_r.at[part, dz, half], target)

    def o_in(part, dz, half):
        source = device(x, yl, core, lax.rem(z + NZ - dz, NZ), half * 2 + 1 - lax.rem(rho, 2))
        into = (near_in, far_in)[part].at[dz, half]
        return remote(into, into, o_s.at[part, dz, half], o_r.at[part, dz, half], source)

    def scatter(part):
        for dz in (4, 3, 5, 2, 6, 1, 7, 0):
            for sp in range(2):
                o_out(part, dz, sp).start()

    pl.semaphore_wait(barrier, len(partners))
    y_out(1).start()
    z_out(2).start()
    a_out(0).start()
    spread(0, 0)
    d_out(3).start()
    a_out(3).start()
    a_out(1).start()
    a_out(2).start()
    tell(0)

    get_mom.wait()
    row = lax.broadcasted_iota(jnp.int32, (8, 128), 0)
    lane = lax.broadcasted_iota(jnp.int32, (8, 128), 1)
    hi_row = rho + (row & 1) * (ahead - rho)
    z_row = z + (lax.shift_right_logical(row, 1) & 1) * (flip(z) - z)
    flat = ((z_row * 4 + hi_row) * 128 + lane).astype(F32)
    plane = jnp.floor((flat + 0.5) * (1.0 / (LEXT * LEXT)))
    line = jnp.floor((flat + 0.5) * (1.0 / LEXT))
    coords = (flat - LEXT * line, line - LEXT * plane, plane)
    for k in range(4):
        turns = sum(mom[k, d].astype(F32) * coords[d] for d in range(3))
        turns = turns - LEXT * jnp.floor((turns + 0.5) * (1.0 / LEXT))
        angle = turns * (TWO_PI / LEXT)
        wave[0, pl.ds(8 * k, 8), :] = jnp.cos(angle)
        wave[1, pl.ds(8 * k, 8), :] = jnp.sin(angle)

    def share(e):
        for far in (1, -1):
            s_copy(far, e, core).start()

    def far_of(e):
        relay_far(e, 0)
        relay_far(e, 1)
        s_copy(2, e, core).start()

    prepare(0)
    a_in(0).wait_recv()
    spread(0, 1)
    g_in(2, 0).wait_recv()
    spread(2, 0)
    g_in(1, 0).wait_recv()
    spread(1, 0)
    for j, i in ((0, 0), (2, 1), (3, 3)):
        z_out(i).start()
        y_out(j).start()
        d_out(j if j < 3 else 1).start()
    s_copy(0, 0, core).start()
    a_in(2).wait_recv()
    spread(2, 1)
    relay(0, 0)
    a_in(1).wait_recv()
    spread(1, 1)
    g_in(3, 0).wait_recv()
    spread(3, 0)
    a_in(3).wait_recv()
    spread(3, 1)
    for e in (2, 1, 3):
        s_copy(0, e, core).start()
    relay(0, 1)
    share(0)
    relay(2, 0)
    relay(1, 0)
    relay(2, 1)
    share(2)
    hear(0)
    tell(1)
    for j in (1, 2, 3):
        g_in(2, j).wait_recv()
    prepare(2)
    relay(1, 1)
    share(1)
    for far in (0, 1, -1):
        whole(0, far)
    multiply_near(0, first=True)
    relay(3, 0)
    relay(3, 1)
    share(3)
    for j in (1, 2, 3):
        g_in(1, j).wait_recv()
    prepare(1)
    far_of(0)
    for far in (0, 1, -1):
        whole(2, far)
    multiply_near(2)
    far_of(2)
    for j in (1, 2, 3):
        g_in(3, j).wait_recv()
    prepare(3)
    far_of(1)
    for far in (0, 1, -1):
        whole(1, far)
    multiply_near(1)
    for far in (0, 1, -1):
        whole(3, far)
    multiply_near(3, last=True)
    hear(1)
    scatter(0)
    far_of(3)
    for e in (0, 2, 1):
        whole(e, 2)
    multiply_far((0, 2, 1), first=True)
    whole(3, 2)
    multiply_far((3,), last=True)
    scatter(1)

    for e in range(NH):
        a_out(e).wait_send()
        for o in range(2):
            x_out(1, e, o).wait_send()
            x_out(-1, e, o).wait_send()
            w_out(e, o).wait_send()
        for far in range(NX):
            s_copy(far, e, core).wait_send()
        y_out(e).wait_send()
        z_out(e).wait_send()
        d_out(e).wait_send()

    for part in range(2):
        for dz in range(NZ):
            for sp in range(2):
                o_out(part, dz, sp).wait_send()

    for part, slots in ((0, 3), (1, 1)):
        totals = [None, None]
        for dz in (0, 1, 7, 2, 6, 3, 5, 4):
            for half in range(2):
                o_in(part, dz, half).wait_recv()
                some = (near_in, far_in)[part][dz, half].astype(F32)
                totals[dz % 2] = some if totals[dz % 2] is None else totals[dz % 2] + some
        for odd in range(2):
            for slot in range(slots):
                far = FAR[3 * part + slot]
                tiles[lax.rem(z + odd, 2), lax.rem(x + far, NX)] = totals[odd][slot]
    low = lax.broadcasted_iota(jnp.int32, (16, 128), 1) < 64
    for r in range(2):
        for v in range(2):
            even, odd = tiles[r, 2 * v], tiles[r, 2 * v + 1]
            out_ref[2 * r, :, pl.ds(128 * v, 128)] = jnp.where(low, even, pltpu.roll(odd, 64, 1))
            out_ref[2 * r + 1, :, pl.ds(128 * v, 128)] = jnp.where(low, pltpu.roll(even, 64, 1), odd)


def shards(modes, momenta):
    dma = pltpu.SemaphoreType.DMA
    return pl.pallas_call(
        kernel,
        out_shape=jax.ShapeDtypeStruct((4, 16, 256), F32),
        in_specs=[
            pl.BlockSpec(memory_space=pl.ANY),
            pl.BlockSpec(memory_space=pl.ANY),
        ],
        out_specs=pl.BlockSpec(memory_space=pltpu.VMEM),
        scratch_shapes=[
            pltpu.VMEM((2, 1, 12, 16, 128), BF16),
            pltpu.SMEM((4, 3), jnp.int32),
            pltpu.VMEM((NH, 64, KEY), BF16),
            pltpu.VMEM((NH, NX, 2, 2, 2, 16, KEY), BF16),
            pltpu.VMEM((NH, 512, KEY), BF16),
            pltpu.VMEM((256, 384), F32),
            pltpu.VMEM((256, 128), F32),
            pltpu.VMEM((2, 32, 128), F32),
            pltpu.VMEM((NZ, 2, 3, 16, 128), BF16),
            pltpu.VMEM((NZ, 2, 3, 16, 128), BF16),
            pltpu.VMEM((NZ, 2, 1, 16, 128), BF16),
            pltpu.VMEM((NZ, 2, 1, 16, 128), BF16),
            pltpu.VMEM((2, NX, 16, 128), F32),
            pltpu.SemaphoreType.REGULAR((2, 2)),
            dma((2,)),
            dma((3, 4)), dma((3, 4)),
            dma((NH,)), dma((NH,)),
            dma((2, NH, 2)), dma((2, NH, 2)),
            dma((NH, 2)), dma((NH, 2)),
            dma((NX, NH)), dma((NX, NH)),
            dma((2, NZ, 2)), dma((2, NZ, 2)),
        ],
        compiler_params=pltpu.CompilerParams(
            collective_id=0, has_side_effects=True, vmem_limit_bytes=56 * 1024 * 1024
        ),
    )(jnp.transpose(modes, (0, 1, 3, 2, 4)), momenta)


def solution(mesh):
    placed = (P(None, None, "blk", None, "site"), P())
    return jax.shard_map(
        shards, mesh=mesh, in_specs=placed, out_specs=P("site", "blk", None), check_vma=False
    )
```

```python
import math

import jax
import jax.numpy as jnp
from jax import lax
from jax.experimental import pallas as pl
from jax.experimental.pallas import tpu as pltpu
from jax.sharding import PartitionSpec as P

LEXT = 48
TWO_PI = 2.0 * math.pi
MESH = pl.DeviceIdType.MESH
F32 = jnp.float32
BF16 = jnp.bfloat16

NX, NZ, NH = 4, 8, 4
FAR = (0, 1, 3, 2)
SLOT = tuple(FAR.index(far) for far in range(NX))
KEY = 768
ROWS = (((1,), (1,)), ((), ()))


def remote(src, dst, send_sem, recv_sem, target):
    return pltpu.make_async_remote_copy(
        src_ref=src, dst_ref=dst, send_sem=send_sem, recv_sem=recv_sem,
        device_id=target, device_id_type=MESH,
    )


def flip(place):
    return place + 1 - 2 * lax.rem(place, 2)


def spin_rows(spin):
    return pl.ds(pl.multiple_of(spin * 16, 16), 16)


def kernel(
    modes_ref, mom_ref, out_ref,
    stage, mom, rows, cols, left, acc, acc_far, wave, near_out, near_in, far_out, far_in, tiles,
    hand, in_s, g_s, g_r, a_s, a_r, x_s, x_r, w_s, w_r, s_s, s_r, o_s, o_r,
):
    blk = lax.axis_index("blk")
    site = lax.axis_index("site")
    x = lax.div(blk, 4)
    yl = lax.rem(lax.div(blk, 2), 2)
    core = lax.rem(blk, 2)
    z = lax.div(site, 4)
    rho = lax.rem(site, 4)

    ahead = lax.rem(rho + 3 + 2 * yl, NH)
    behind = lax.rem(rho + 1 + 2 * yl, NH)

    def z_of(e):
        return flip(z) if e // 2 else z

    def spin_of(e):
        hi = lax.rem(rho + e, 2)
        return (1 - hi) * 2 + lax.rem(z_of(e), 2)

    spin = spin_of(0)

    def device(x, yl, core, z, hi):
        return (x * 4 + yl * 2 + core, z * 4 + hi)

    def lane_of(o):
        return yl if o == 0 else 1 - yl

    barrier = pltpu.get_barrier_semaphore()
    partners = [device(x, yl, 1 - core, z, rho)]
    partners += [device(lax.rem(x + dx, NX), yl, core, z, rho) for dx in (1, NX - 1)]
    partners += [device(x, 1 - yl, core, z_of(e), ahead if e % 2 else rho) for e in range(NH)]
    partners += [device(x, yl, core, flip(z), hi) for hi in (ahead, behind)]
    along_z = [device(x, yl, core, lax.rem(z + dz, NZ), rho) for dz in (2, NZ - 2, 1, NZ - 1)]
    along_y = [device(x, yl, core, z, lax.rem(rho + dh, NH)) for dh in (1, NH - 1)]
    partners += along_z + along_y
    for target in partners:
        pl.semaphore_signal(barrier, inc=1, device_id=target, device_id_type=MESH)
    get_modes = pltpu.make_async_copy(modes_ref, stage, in_s.at[0])
    get_modes.start()
    get_mom = pltpu.make_async_copy(mom_ref, mom, in_s.at[1])
    get_mom.start()

    get_modes.wait()
    for c in range(2):
        for s in range(4):
            for a in range(3):
                rows[0, pl.ds(16 * s, 16), pl.ds((c * 3 + a) * 128, 128)] = stage[c, 0, 3 * s + a]

    def gather(e, spin_e, e_from, to):
        return remote(
            rows.at[e_from, spin_rows(spin_e), :], rows.at[e, spin_rows(spin_e), :],
            g_s.at[e - 1, spin_e], g_r.at[e - 1, spin_e], to,
        )

    def y_out(j):
        return gather(1, spin_of(j), 0, device(x, yl, core, z, behind))

    def z_out(j):
        return gather(2, spin_of(j), 0, device(x, yl, core, flip(z), rho))

    def d_out(j):
        return gather(3, spin_of(j), 0, device(x, yl, core, flip(z), behind))

    def g_in(e, j):
        to = device(x, yl, core, flip(z), rho) if e > 1 else device(x, yl, core, z, ahead)
        return gather(e, spin_of(j), e, to)

    def piece(e, far, o, side):
        return cols.at[e, SLOT[far % NX], 0, lane_of(o), side]

    def a_out(e):
        to = device(x, 1 - yl, core, z_of(e), ahead if e % 2 else rho)
        return remote(rows.at[0, spin_rows(spin_of(e)), :], piece(e, 0, 0, core), a_s.at[e], a_r.at[e], to)

    def a_in(e):
        into = piece(e, 0, 1, core)
        return remote(into, into, a_s.at[e], a_r.at[e], device(x, 1 - yl, core, z_of(e), ahead if e % 2 else rho))

    def along_x(dx):
        return device(lax.rem(x + dx + NX, NX), yl, core, z, rho)

    def x_out(dx, e, o):
        at = (dx + 1) // 2
        return remote(
            piece(e, 0, o, core), piece(e, -dx, o, core), x_s.at[at, e, o], x_r.at[at, e, o], along_x(dx)
        )

    def x_in(dx, e, o):
        at, into = (dx + 1) // 2, piece(e, -dx, o, core)
        return remote(into, into, x_s.at[at, e, o], x_r.at[at, e, o], along_x(dx))

    def w_out(e, o):
        dx = 1 - 2 * o
        return remote(piece(e, -dx, o, core), piece(e, 2, o, core), w_s.at[e, o], w_r.at[e, o], along_x(dx))

    def w_in(e, o):
        into = piece(e, 2, o, core)
        return remote(into, into, w_s.at[e, o], w_r.at[e, o], along_x(1 - 2 * o))

    def s_copy(far, e, side):
        at = SLOT[far % NX]
        both = cols.at[e, at, 0, :, side]
        return remote(both, both, s_s.at[at, e], s_r.at[at, e], device(x, yl, 1 - core, z, rho))

    def spread(e, o):
        if o == 0:
            cols[e, 0, 0, yl, core] = rows[e, spin_rows(spin), :]
        x_out(1, e, o).start()
        x_out(-1, e, o).start()

    def relay(e, o):
        x_in(1, e, o).wait_recv()
        x_in(-1, e, o).wait_recv()
        w_out(e, o).start()

    def relay_far(e, o):
        w_in(e, o).wait_recv()

    def whole(e, far):
        s_copy(far, e, 1 - core).wait_recv()
        at = SLOT[far % NX]
        for l in range(2):
            for side in range(2):
                for a in range(3):
                    cols[e, at, 1, l, side, :, pl.ds(a * 128, 128)] = cols[e, at, 0, l, side, :, pl.ds((3 + a) * 128, 128)]
                    cols[e, at, 1, l, side, :, pl.ds((3 + a) * 128, 128)] = -cols[e, at, 0, l, side, :, pl.ds(a * 128, 128)]

    def prepare(e):
        for k in range(4):
            cos = wave[0, pl.ds(8 * k + e, 1), :]
            sin = wave[1, pl.ds(8 * k + e, 1), :]
            for s in range(4):
                for a in range(3):
                    ur = rows[e, pl.ds(16 * s, 16), pl.ds(a * 128, 128)].astype(F32)
                    ui = rows[e, pl.ds(16 * s, 16), pl.ds((3 + a) * 128, 128)].astype(F32)
                    for c, value in enumerate((ur * cos - ui * sin, ui * cos + ur * sin)):
                        high = value.astype(BF16)
                        at, lanes = k * 64 + s * 16, pl.ds((3 * c + a) * 128, 128)
                        left[e, pl.ds(at, 16), lanes] = high
                        left[e, pl.ds(256 + at, 16), lanes] = (value - high.astype(F32)).astype(BF16)

    def product(e, right):
        part = lax.dot_general(left[e], right, ROWS, preferred_element_type=F32)
        return part[:256] + part[256:]

    def put(out, sums, slots):
        for k in range(4):
            for s in range(4):
                for slot in range(slots):
                    tile = sums[64 * k + 16 * s:64 * k + 16 * s + 16, 128 * slot:128 * slot + 128]
                    out[2 * k + s // 2, s % 2, slot] = tile.astype(BF16)

    def multiply_near(e, first=False, last=False):
        part = product(e, cols[e, pl.ds(0, 3)].reshape(384, KEY))
        if not first:
            part += acc[...]
        if last:
            put(near_out, part, 3)
        else:
            acc[...] = part

    def multiply_far(es, first=False, last=False):
        part = None if first else acc_far[...]
        for e in es:
            more = product(e, cols[e, 3].reshape(128, KEY))
            part = more if part is None else part + more
        if last:
            put(far_out, part, 1)
        else:
            acc_far[...] = part

    def tell(turn):
        for side, to in enumerate(along_y if turn else along_z[:2]):
            pl.semaphore_signal(hand.at[turn, side], inc=1, device_id=to, device_id_type=MESH)

    def hear(turn):
        for side in range(2):
            pl.semaphore_wait(hand.at[turn, side], 1)

    def o_out(part, dz, sp):
        to = lax.rem(z + dz, NZ)
        half = lax.div(rho, 2)
        target = device(x, yl, core, to, sp * 2 + 1 - lax.rem(rho, 2))
        src, dst = ((near_out, near_in), (far_out, far_in))[part]
        return remote(src.at[to, sp], dst.at[dz, half], o_s.at[part, dz, sp], o_r.at[part, dz, half], target)

    def o_in(part, dz, half):
        source = device(x, yl, core, lax.rem(z + NZ - dz, NZ), half * 2 + 1 - lax.rem(rho, 2))
        into = (near_in, far_in)[part].at[dz, half]
        return remote(into, into, o_s.at[part, dz, half], o_r.at[part, dz, half], source)

    def scatter(part):
        for dz in (4, 3, 5, 2, 6, 1, 7, 0):
            for sp in range(2):
                o_out(part, dz, sp).start()

    get_mom.wait()
    row = lax.broadcasted_iota(jnp.int32, (8, 128), 0)
    lane = lax.broadcasted_iota(jnp.int32, (8, 128), 1)
    hi_row = rho + (row & 1) * (ahead - rho)
    z_row = z + (lax.shift_right_logical(row, 1) & 1) * (flip(z) - z)
    flat = ((z_row * 4 + hi_row) * 128 + lane).astype(F32)
    plane = jnp.floor((flat + 0.5) * (1.0 / (LEXT * LEXT)))
    line = jnp.floor((flat + 0.5) * (1.0 / LEXT))
    coords = (flat - LEXT * line, line - LEXT * plane, plane)
    for k in range(4):
        turns = sum(mom[k, d].astype(F32) * coords[d] for d in range(3))
        turns = turns - LEXT * jnp.floor((turns + 0.5) * (1.0 / LEXT))
        angle = turns * (TWO_PI / LEXT)
        wave[0, pl.ds(8 * k, 8), :] = jnp.cos(angle)
        wave[1, pl.ds(8 * k, 8), :] = jnp.sin(angle)

    def share(e):
        for far in (1, -1):
            s_copy(far, e, core).start()

    pl.semaphore_wait(barrier, len(partners))
    y_out(1).start()
    z_out(2).start()
    a_out(0).start()
    spread(0, 0)
    d_out(3).start()
    a_out(3).start()
    a_out(1).start()
    a_out(2).start()
    tell(0)

    def far_of(e):
        relay_far(e, 0)
        relay_far(e, 1)
        s_copy(2, e, core).start()

    prepare(0)
    a_in(0).wait_recv()
    spread(0, 1)
    g_in(2, 0).wait_recv()
    spread(2, 0)
    g_in(1, 0).wait_recv()
    spread(1, 0)
    for j, i in ((0, 0), (2, 1), (3, 3)):
        z_out(i).start()
        y_out(j).start()
        d_out(j if j < 3 else 1).start()
    s_copy(0, 0, core).start()
    a_in(2).wait_recv()
    spread(2, 1)
    relay(0, 0)
    a_in(1).wait_recv()
    spread(1, 1)
    g_in(3, 0).wait_recv()
    spread(3, 0)
    a_in(3).wait_recv()
    spread(3, 1)
    for e in (2, 1, 3):
        s_copy(0, e, core).start()
    relay(0, 1)
    share(0)
    relay(2, 0)
    relay(1, 0)
    relay(2, 1)
    share(2)
    hear(0)
    tell(1)
    for j in (1, 2, 3):
        g_in(2, j).wait_recv()
    prepare(2)
    relay(1, 1)
    share(1)
    for far in (0, 1, -1):
        whole(0, far)
    multiply_near(0, first=True)
    relay(3, 0)
    relay(3, 1)
    share(3)
    for j in (1, 2, 3):
        g_in(1, j).wait_recv()
    prepare(1)
    far_of(0)
    for far in (0, 1, -1):
        whole(2, far)
    multiply_near(2)
    far_of(2)
    for j in (1, 2, 3):
        g_in(3, j).wait_recv()
    prepare(3)
    far_of(1)
    for far in (0, 1, -1):
        whole(1, far)
    multiply_near(1)
    for far in (0, 1, -1):
        whole(3, far)
    multiply_near(3, last=True)
    hear(1)
    scatter(0)
    far_of(3)
    for e in (0, 2, 1):
        whole(e, 2)
    multiply_far((0, 2, 1), first=True)
    whole(3, 2)
    multiply_far((3,), last=True)
    scatter(1)

    for e in range(NH):
        a_out(e).wait_send()
        for o in range(2):
            x_out(1, e, o).wait_send()
            x_out(-1, e, o).wait_send()
            w_out(e, o).wait_send()
        for far in range(NX):
            s_copy(far, e, core).wait_send()
        y_out(e).wait_send()
        z_out(e).wait_send()
        d_out(e).wait_send()

    for part in range(2):
        for dz in range(NZ):
            for sp in range(2):
                o_out(part, dz, sp).wait_send()

    for part, slots in ((0, 3), (1, 1)):
        totals = [None, None]
        for dz in (0, 1, 7, 2, 6, 3, 5, 4):
            for half in range(2):
                o_in(part, dz, half).wait_recv()
                some = (near_in, far_in)[part][dz, half].astype(F32)
                totals[dz % 2] = some if totals[dz % 2] is None else totals[dz % 2] + some
        for odd in range(2):
            for slot in range(slots):
                far = FAR[3 * part + slot]
                tiles[lax.rem(z + odd, 2), lax.rem(x + far, NX)] = totals[odd][slot]
    low = lax.broadcasted_iota(jnp.int32, (16, 128), 1) < 64
    for r in range(2):
        for v in range(2):
            even, odd = tiles[r, 2 * v], tiles[r, 2 * v + 1]
            out_ref[2 * r, :, pl.ds(128 * v, 128)] = jnp.where(low, even, pltpu.roll(odd, 64, 1))
            out_ref[2 * r + 1, :, pl.ds(128 * v, 128)] = jnp.where(low, pltpu.roll(even, 64, 1), odd)


def shards(modes, momenta):
    dma = pltpu.SemaphoreType.DMA
    return pl.pallas_call(
        kernel,
        out_shape=jax.ShapeDtypeStruct((4, 16, 256), F32),
        in_specs=[
            pl.BlockSpec(memory_space=pl.ANY),
            pl.BlockSpec(memory_space=pl.ANY),
        ],
        out_specs=pl.BlockSpec(memory_space=pltpu.VMEM),
        scratch_shapes=[
            pltpu.VMEM((2, 1, 12, 16, 128), BF16),
            pltpu.SMEM((4, 3), jnp.int32),
            pltpu.VMEM((NH, 64, KEY), BF16),
            pltpu.VMEM((NH, NX, 2, 2, 2, 16, KEY), BF16),
            pltpu.VMEM((NH, 512, KEY), BF16),
            pltpu.VMEM((256, 384), F32),
            pltpu.VMEM((256, 128), F32),
            pltpu.VMEM((2, 32, 128), F32),
            pltpu.VMEM((NZ, 2, 3, 16, 128), BF16),
            pltpu.VMEM((NZ, 2, 3, 16, 128), BF16),
            pltpu.VMEM((NZ, 2, 1, 16, 128), BF16),
            pltpu.VMEM((NZ, 2, 1, 16, 128), BF16),
            pltpu.VMEM((2, NX, 16, 128), F32),
            pltpu.SemaphoreType.REGULAR((2, 2)),
            dma((2,)),
            dma((3, 4)), dma((3, 4)),
            dma((NH,)), dma((NH,)),
            dma((2, NH, 2)), dma((2, NH, 2)),
            dma((NH, 2)), dma((NH, 2)),
            dma((NX, NH)), dma((NX, NH)),
            dma((2, NZ, 2)), dma((2, NZ, 2)),
        ],
        compiler_params=pltpu.CompilerParams(
            collective_id=0, has_side_effects=True, vmem_limit_bytes=56 * 1024 * 1024
        ),
    )(jnp.transpose(modes, (0, 1, 3, 2, 4)), momenta)


def solution(mesh):
    placed = (P(None, None, "blk", None, "site"), P())
    return jax.shard_map(
        shards, mesh=mesh, in_specs=placed, out_specs=P("site", "blk", None), check_vma=False
    )
```
